32 devices in a mesh: ctx: 2 (over core), fsdp: 16 (over z, y, x).
Axes of the slice: x: 2, y: 2, z: 4, core: 2. Of those that a mesh axis runs over, the one named last changes fastest.
Arguments:
- tokens: bfloat16 [64, 1024, 1024], P('fsdp', 'ctx'), may hold values from -6 to 6
- cotangent: bfloat16 [64, 1024, 1024], P('fsdp', 'ctx'), may hold values from -6 to 6
- lengths: int32 [64], P('fsdp'), may hold values from 256 to 1024, as said below
- norm_gain: bfloat16 [1024], P('fsdp'), may hold values from 0.099609375 to 1.8984375
- query_weight: bfloat16 [1024, 1024], P('fsdp'), may hold values from -0.078125 to 0.078125
- key_weight: bfloat16 [1024, 1024], P('fsdp'), may hold values from -0.078125 to 0.078125
- value_weight: bfloat16 [1024, 1024], P('fsdp'), may hold values from -0.1875 to 0.1875
- output_weight: bfloat16 [1024, 1024], P('fsdp'), may hold values from -1.5 to 1.5
- ffn_gain: bfloat16 [1024], P('fsdp'), may hold values from 0.099609375 to 1.8984375
- inner_weight: bfloat16 [1024, 4096], P('fsdp'), may hold values from -0.1875 to 0.1875
- outer_weight: bfloat16 [4096, 1024], P('fsdp'), may hold values from -0.09375 to 0.09375
- bias_table: bfloat16 [32, 16], P('fsdp'), may hold values from -4 to 4
Outputs:
- layer_out: bfloat16 [64, 1024, 1024], P('fsdp', 'ctx')
- token_grad: float32 [64, 1024, 1024], P('fsdp', 'ctx')
- norm_gain_grad: float32 [1024], P('fsdp')
- query_grad: float32 [1024, 1024], P('fsdp')
- key_grad: float32 [1024, 1024], P('fsdp')
- value_grad: float32 [1024, 1024], P('fsdp')
- output_grad: float32 [1024, 1024], P('fsdp')
- ffn_gain_grad: float32 [1024], P('fsdp')
- inner_grad: float32 [1024, 4096], P('fsdp')
- outer_grad: float32 [4096, 1024], P('fsdp')
- table_grad: float32 [32, 16], P('fsdp')
The draws below stay inside these ranges and needn't reach their ends.
Inputs may be any that keep to these rules, and one draw needn't show every extreme that they name: The first lengths[s] positions of sequence s are live; one sequence of each index of fsdp has all 1024.
All inputs are finite; a program needn't handle non-finite values.
Results may differ from the reference program's by a relative error of at most 0.023.
Values may be sent and summed in bfloat16 or wider, within the bound.
A program may use at most 472 MiB of HBM per device.

```python
import math
import jax
import jax.numpy as jnp
import numpy as np
from jax import lax

D = 1024
FF = 4096
HEADS = 16
BUCKETS = 32
LEN = 1024
MB = 4
SEQ_MB = 1
SEQS = 64


def draw_lengths(key, part):
    key = jax.random.fold_in(key, 11)
    group_size = MB * SEQ_MB
    group_count = SEQS // group_size
    key_base, key_full, key_short = jax.random.split(key, 3)
    drawn = jax.random.randint(key_base, (group_count, group_size), LEN // 4, LEN + 1)
    full_at = jax.random.randint(key_full, (group_count, 1), 0, group_size)
    short_at = (full_at + jax.random.randint(key_short, (group_count, 1), 1, group_size)) % group_size
    slot_index = jnp.arange(group_size)[None, :]
    drawn = jnp.where(slot_index == full_at, LEN, drawn)
    drawn = jnp.where(slot_index == short_at, LEN // 4, drawn)
    return drawn.reshape(SEQS).astype(jnp.int32)


def steps_of(key, dims, pieces, low, high):
    loudness = 1.0
    for dim, parts in pieces:
        draws = jax.random.uniform(jax.random.fold_in(jax.random.fold_in(key, 6), dim), (parts,), jnp.float32, low / len(pieces), high / len(pieces))
        loudness = loudness * jnp.repeat(jnp.exp(draws), dims[dim] // parts).reshape((-1,) + (1,) * (len(dims) - 1 - dim))
    return loudness


def bell_draw(key, shape, spread, most, cuts=(), kind=jnp.bfloat16):
    level = steps_of(key, shape, cuts, -0.22, 0.18) if cuts else 1.0
    entries = jax.random.normal(key, shape, jnp.float32) * spread * level
    return jnp.minimum(jnp.maximum(entries, -most), most).astype(kind)


def setup_inputs(seed: int = 0) -> dict:
    key_of = jax.random.split(jax.random.key(seed), 13)
    return {
        "tokens": bell_draw(key_of[0], (SEQS, LEN, D), 1.0, 6.0, ((0, 16), (1, 2))),
        "cotangent": bell_draw(key_of[1], (SEQS, LEN, D), 1.0, 6.0, ((0, 16), (1, 2))),
        "lengths": draw_lengths(jax.random.fold_in(key_of[12], 71), 0),
        "norm_gain": jnp.clip(1.0 + 0.18 * jax.random.normal(key_of[3], (D,), jnp.float32), 0.099609375, 1.8984375).astype(jnp.bfloat16),
        "query_weight": bell_draw(key_of[4], (D, D), (5 * D) ** -0.5, 0.078125, ((0, 16),)),
        "key_weight": bell_draw(key_of[5], (D, D), (5 * D) ** -0.5, 0.078125, ((0, 16),)),
        "value_weight": bell_draw(key_of[6], (D, D), D ** -0.5, 0.1875, ((0, 16),)),
        "output_weight": bell_draw(key_of[7], (D, D), (max(D // 64, 1)) ** -0.5, 1.5, ((0, 16),)),
        "ffn_gain": jnp.clip(1.0 + 0.18 * jax.random.normal(key_of[8], (D,), jnp.float32), 0.099609375, 1.8984375).astype(jnp.bfloat16),
        "inner_weight": bell_draw(key_of[9], (D, FF), D ** -0.5, 0.1875, ((0, 16),)),
        "outer_weight": bell_draw(key_of[10], (FF, D), FF ** -0.5, 0.09375, ((0, 16),)),
        "bias_table": bell_draw(key_of[11], (BUCKETS, HEADS), 1.0, 4.0, ((0, 16),)),
    }


eps_norm = 1e-06
neg_large = -1e+30
gelu_coef = 0.7978845608028654

@jax.custom_vjp
def low(v):
    return lax.optimization_barrier(v.astype(jnp.bfloat16)).astype(jnp.float32)

@jax.custom_vjp
def low_back(v):
    return v

def low_keep(v):
    return (low(v), None)

def low_pass(kept, grad):
    return (grad,)

def back_keep(v):
    return (v, None)

def back_low(kept, grad):
    return (low(grad),)
low.defvjp(low_keep, low_pass)
low_back.defvjp(back_keep, back_low)

def bucket_edges():
    distance = np.arange(1, 512)
    scaled = 8 + np.floor(np.log(distance / 8.0) / np.log(16.0) * 8.0)
    bucket_level = np.where(distance < 8, distance, np.minimum(15, scaled))
    return np.array([distance[bucket_level >= target][0] for target in range(1, 16)], np.int32)

def bucket_levels(query_pos, key_pos):
    offset = key_pos[None, :] - query_pos[:, None]
    magnitude = jnp.abs(offset)
    bucket_bound = jnp.asarray(bucket_edges())
    bucket_level = lax.optimization_barrier(jnp.sum((magnitude[:, :, None] >= bucket_bound).astype(jnp.int32), axis=2))
    return bucket_level + 16 * (offset > 0).astype(jnp.int32)

def root_norm(row_values, gain_values):
    inv_root = lax.rsqrt(lax.optimization_barrier(jnp.mean(row_values * row_values, axis=-1, keepdims=True)) + eps_norm)
    return row_values * inv_root * gain_values

def smooth_gelu(row_values):
    return 0.5 * row_values * (1.0 + jnp.tanh(gelu_coef * (row_values + 0.044715 * row_values * row_values * row_values)))

def dense_hi(row_values, weight):
    return jnp.dot(row_values, weight, precision=lax.Precision.HIGHEST, preferred_element_type=jnp.float32)

def forward(params, token_rows, seq_lengths, levels):
    norm_gain, query_weight, key_weight, value_weight, output_weight, ffn_gain, inner_weight, outer_weight, bias_table = params
    seq_count, seq_len, model_width = token_rows.shape
    head_count = bias_table.shape[1]
    head_dim = model_width // head_count
    flat = token_rows.reshape(seq_count * seq_len, model_width)
    normed = low(root_norm(flat, norm_gain))
    queries = low(low_back(dense_hi(normed, query_weight)))
    key_rows = low(low_back(dense_hi(normed, key_weight)))
    value_rows = low(low_back(dense_hi(normed, value_weight)))
    bias_full = jnp.transpose(jnp.take(bias_table, levels, axis=0), (2, 0, 1))
    positions = jnp.arange(seq_len, dtype=jnp.int32)

    def one_sequence(inputs):
        query_seq, key_seq, value_seq, seq_length = inputs
        query_four = query_seq.reshape(seq_len, head_count, head_dim)
        key_four = key_seq.reshape(seq_len, head_count, head_dim)
        value_four = value_seq.reshape(seq_len, head_count, head_dim)
        raw_scores = jnp.einsum('ihd,jhd->hij', query_four, key_four, precision=lax.Precision.HIGHEST)
        scores = low_back(raw_scores + bias_full)
        live_keys = positions < seq_length
        scores = jnp.where(live_keys[None, None, :], scores, neg_large)
        shifted = scores - lax.optimization_barrier(jnp.max(scores, axis=-1, keepdims=True))
        exp_scores = jnp.exp(shifted)
        attn_probs = exp_scores / lax.optimization_barrier(jnp.sum(exp_scores, axis=-1, keepdims=True))
        mixed = jnp.einsum('hij,jhd->ihd', low(attn_probs), value_four, precision=lax.Precision.HIGHEST)
        return mixed.reshape(seq_len, model_width)
    mixed_all = lax.map(jax.checkpoint(one_sequence), (queries.reshape(seq_count, seq_len, model_width), key_rows.reshape(seq_count, seq_len, model_width), value_rows.reshape(seq_count, seq_len, model_width), seq_lengths))
    mixed_all = low(low_back(mixed_all.reshape(seq_count * seq_len, model_width)))
    attn_out = low_back(dense_hi(mixed_all, output_weight))
    residual = flat + attn_out
    normed_ffn = low(root_norm(residual, ffn_gain))
    inner_act = low_back(dense_hi(normed_ffn, inner_weight))
    hidden = low(smooth_gelu(inner_act))
    outer_act = low_back(dense_hi(hidden, outer_weight))
    return (residual + outer_act).reshape(seq_count, seq_len, model_width)

def reference(tokens, cotangent, lengths, norm_gain, query_weight, key_weight, value_weight, output_weight, ffn_gain, inner_weight, outer_weight, bias_table):
    params = tuple((weight.astype(jnp.float32) for weight in (norm_gain, query_weight, key_weight, value_weight, output_weight, ffn_gain, inner_weight, outer_weight, bias_table)))
    positions = jnp.arange(LEN, dtype=jnp.int32)
    levels = bucket_levels(positions, positions)
    group_size = math.gcd(SEQS, max(1, 4096 // LEN))
    group_count = SEQS // group_size
    token_groups = tokens.reshape(group_count, group_size, LEN, D)
    cot_groups = cotangent.reshape(group_count, group_size, LEN, D)
    length_groups = lengths.reshape(group_count, group_size)

    def group_step(totals, inputs):
        token_group, cot_group, length_group = inputs
        token_rows = token_group.astype(jnp.float32)

        def run_layer(row_values, weights):
            return forward(weights, row_values, length_group, levels)
        layer_rows, pullback = jax.vjp(run_layer, token_rows, params)
        live_rows = (positions[None, :] < length_group[:, None]).astype(jnp.float32)[:, :, None]
        token_grad, weight_grads = pullback(cot_group.astype(jnp.float32) * live_rows)
        totals = tuple((total_part + grad_part for total_part, grad_part in zip(totals, weight_grads)))
        return (totals, (layer_rows.astype(jnp.bfloat16), token_grad))
    zeros = tuple((jnp.zeros(weight.shape, jnp.float32) for weight in params))
    totals, outputs = lax.scan(group_step, zeros, (token_groups, cot_groups, length_groups))
    layer_out = outputs[0].reshape(SEQS, LEN, D)
    token_grad = outputs[1].reshape(SEQS, LEN, D)
    return (layer_out, token_grad, totals[0], totals[1], totals[2], totals[3], totals[4], totals[5], totals[6], totals[7], totals[8])
```

```python
import functools

import jax
import jax.numpy as jnp
import numpy as np
from jax import lax
from jax.experimental import pallas as pl
from jax.experimental.pallas import tpu as pltpu
from jax.sharding import PartitionSpec as P

LOG2E = 1.4426950408889634
LN2 = 0.6931471805599453
NEG = -1e30
TILE = 256
QT = 512
HEAD_DIM = 64
EPS = 1e-6
GELU = 0.7978845608028654
CUBIC = 0.044715


def dot(a, b, ca, cb, precision=None):
    return lax.dot_general(a, b, (((ca,), (cb,)), ((), ())), precision=precision,
                           preferred_element_type=jnp.float32)

def attend_kernel(len_ref, tvec_ref, q_ref, k_ref, v_ref, o_ref, lse_ref, strip_ref, *, seq_len, head_dim):
    heads = q_ref.shape[-1] // head_dim
    blocks = seq_len // TILE
    far = seq_len - QT

    @pl.when(pl.program_id(1) == 0)
    def _():
        for h in range(heads):
            wide = jnp.broadcast_to(tvec_ref[0, h : h + 1, :], (QT, tvec_ref.shape[-1]))
            strip_ref[h] = pltpu.roll(wide, 0, 1, stride=1, stride_axis=0)

    live = len_ref[pl.program_id(1)]
    lane = lax.broadcasted_iota(jnp.int32, (1, q_ref.shape[-1]), 1) // head_dim
    column = lax.broadcasted_iota(jnp.int32, (1, TILE), 1)

    def with_blocks(used):
        top = TILE * used
        kept = [lane == h for h in range(heads)]
        keys = [jnp.where(kept[h], k_ref[0, 0:top, :], 0) for h in range(heads)]
        values = [jnp.where(kept[h], v_ref[0, 0:top, :], 1) for h in range(heads)]

        def query_tile(a, carry):
            here = pl.ds(pl.multiple_of(a * QT, QT), QT)
            q = q_ref[0, here, :]
            total = None
            for h in range(heads):
                at = pl.ds(pl.multiple_of(far - QT * a, TILE), top)
                scores = dot(q, keys[h], 1, 1) + strip_ref[h, :, at]
                last = jnp.where(column + (top - TILE) < live, scores[:, top - TILE :], NEG)
                scores = jnp.concatenate([scores[:, : top - TILE], last], axis=1) if used > 1 else last
                peak = jnp.max(scores, axis=1, keepdims=True)
                probs = jnp.exp2(scores - peak).astype(jnp.bfloat16)
                out = dot(probs, values[h], 1, 0)
                mass = pltpu.roll(out, head_dim, 1)
                out = out * (1.0 / mass)
                total = out if total is None else jnp.where(kept[h], out, total)
                lse = peak + jnp.log2(mass)
                lse_ref[0, 0, h : h + 1, here] = jnp.transpose(lse)[h * head_dim : h * head_dim + 1, :]
            o_ref[0, here, :] = total.astype(jnp.bfloat16)
            return carry

        lax.fori_loop(0, seq_len // QT, query_tile, 0, unroll=True)

    for used in range(1, blocks + 1):
        pl.when((live + TILE - 1) // TILE == used)(functools.partial(with_blocks, used))


def attend(lengths, tvec, q, k, v, head_dim):
    seqs, seq_len, width = q.shape
    pairs = width // 128
    heads = 128 // head_dim
    strip = tvec.shape[-1]
    block = pl.BlockSpec((1, seq_len, 128), lambda p, s, n: (s, 0, p))
    return pl.pallas_call(
        functools.partial(attend_kernel, seq_len=seq_len, head_dim=head_dim),
        grid_spec=pltpu.PrefetchScalarGridSpec(
            num_scalar_prefetch=1, grid=(pairs, seqs),
            in_specs=[pl.BlockSpec((1, heads, strip), lambda p, s, n: (p, 0, 0)), block, block, block],
            out_specs=[block, pl.BlockSpec((1, 1, heads, seq_len), lambda p, s, n: (p, s, 0, 0))],
            scratch_shapes=[pltpu.VMEM((heads, QT, strip), jnp.float32)]),
        out_shape=[jax.ShapeDtypeStruct(q.shape, jnp.bfloat16), jax.ShapeDtypeStruct((pairs, seqs, heads, seq_len), jnp.float32)],
        compiler_params=pltpu.CompilerParams(vmem_limit_bytes=48 << 20),
        cost_estimate=pl.CostEstimate(flops=4 * seqs * width * seq_len * seq_len, bytes_accessed=8 * seqs * seq_len * width, transcendentals=0),
        name="attend",
    )(lengths, tvec, q, k, v)


def unattend_kernel(len_ref, tvec_ref, q_ref, k_ref, v_ref, o_ref, do_ref, lse_ref, dq_ref, dk_ref, dv_ref, dt_ref,
                    strip_ref, sums_ref, dk_acc, dv_acc, *, seq_len, head_dim):
    heads = q_ref.shape[-1] // head_dim
    blocks = seq_len // TILE
    far = seq_len - TILE
    bands = (2 * blocks - 1) * TILE

    @pl.when(pl.program_id(1) == 0)
    def _():
        for h in range(heads):
            wide = jnp.broadcast_to(tvec_ref[0, h : h + 1, :], (TILE, tvec_ref.shape[-1]))
            wide = pltpu.roll(wide, 0, 1, stride=1, stride_axis=0)
            for b in range(2 * blocks - 1):
                strip_ref[TILE * b : TILE * (b + 1), TILE * h : TILE * (h + 1)] = jnp.transpose(wide[:, TILE * b : TILE * (b + 1)])
        sums_ref[...] = jnp.zeros_like(sums_ref)

    live = len_ref[pl.program_id(1)]
    lane = lax.broadcasted_iota(jnp.int32, (1, q_ref.shape[-1]), 1) // head_dim
    row = lax.broadcasted_iota(jnp.int32, (TILE, 1), 0)
    kept = [lane == h for h in range(heads)]

    def with_blocks(used):
        top = TILE * used
        dk_acc[0:top, :] = jnp.zeros((top, dk_acc.shape[1]), jnp.float32)
        dv_acc[0:top, :] = jnp.zeros((top, dv_acc.shape[1]), jnp.float32)

        def query_tile(a, carry):
            here = pl.ds(pl.multiple_of(a * TILE, TILE), TILE)
            q = q_ref[0, here, :]
            do = do_ref[0, here, :]
            product = jnp.transpose(do.astype(jnp.float32) * o_ref[0, here, :].astype(jnp.float32))
            qs = jnp.concatenate([jnp.where(kept[h], q, 0) for h in range(heads)], axis=0)
            dos = jnp.concatenate([jnp.where(kept[h], do, 0) for h in range(heads)], axis=0)
            delta = jnp.concatenate([jnp.sum(product[h * head_dim : (h + 1) * head_dim], axis=0, keepdims=True) for h in range(heads)], axis=1)
            lse = jnp.concatenate([lse_ref[0, 0, h : h + 1, here] for h in range(heads)], axis=1)
            at = pl.ds(pl.multiple_of(far - TILE * a, TILE), top)
            kb = k_ref[0, 0:top, :]
            vb = v_ref[0, 0:top, :]
            p = jnp.exp2(dot(kb, qs, 1, 1) + strip_ref[at, :] - lse)
            last = jnp.where(row + (top - TILE) < live, p[top - TILE :], 0.0)
            p = jnp.concatenate([p[: top - TILE], last], axis=0) if used > 1 else last
            ds = p * (dot(vb, dos, 1, 1) - delta)
            sums_ref[at, :] += ds
            p = p.astype(jnp.bfloat16)
            ds = ds.astype(jnp.bfloat16)
            dv_acc[0:top, :] += dot(p, dos, 1, 0)
            dk_acc[0:top, :] += dot(ds, qs, 1, 0)
            dq = dot(ds, kb, 0, 0)
            dq_total = dq[0:TILE]
            for h in range(1, heads):
                dq_total = jnp.where(kept[h], dq[TILE * h : TILE * (h + 1)], dq_total)
            dq_ref[0, here, :] = (dq_total * LN2).astype(jnp.bfloat16)
            return carry

        lax.fori_loop(0, used, query_tile, 0)
        dk_ref[0, 0:top, :] = dk_acc[0:top, :].astype(jnp.bfloat16)
        dv_ref[0, 0:top, :] = dv_acc[0:top, :].astype(jnp.bfloat16)
        if used < blocks:
            zeros = jnp.zeros((seq_len - top, q_ref.shape[-1]), jnp.bfloat16)
            dq_ref[0, top:, :] = zeros
            dk_ref[0, top:, :] = zeros
            dv_ref[0, top:, :] = zeros

    for used in range(1, blocks + 1):
        pl.when((live + TILE - 1) // TILE == used)(functools.partial(with_blocks, used))

    @pl.when(pl.program_id(1) == pl.num_programs(1) - 1)
    def _():
        wide = dt_ref.shape[-1]
        for h in range(heads):
            turned = jnp.concatenate([jnp.transpose(sums_ref[TILE * b : TILE * (b + 1), TILE * h : TILE * (h + 1)]) for b in range(2 * blocks - 1)]
                                     + [jnp.zeros((TILE, wide - bands), jnp.float32)], axis=1)
            group = turned[0:8]
            for g in range(1, TILE // 8):
                group = group + pltpu.roll(turned[8 * g : 8 * (g + 1)], wide - 8 * g, 1)
            diagonal = group[0:1]
            for s in range(1, 8):
                diagonal = diagonal + pltpu.roll(group[s : s + 1], wide - s, 1)
            dt_ref[0, h : h + 1, :] = diagonal


def unattend(lengths, tvec, q, k, v, o, do, lse, head_dim):
    seqs, seq_len, width = q.shape
    pairs = width // 128
    heads = 128 // head_dim
    strip = tvec.shape[-1]
    bands = 2 * seq_len - TILE
    block = pl.BlockSpec((1, seq_len, 128), lambda p, s, n: (s, 0, p))
    vec = pl.BlockSpec((1, heads, strip), lambda p, s, n: (p, 0, 0))
    return pl.pallas_call(
        functools.partial(unattend_kernel, seq_len=seq_len, head_dim=head_dim),
        grid_spec=pltpu.PrefetchScalarGridSpec(
            num_scalar_prefetch=1, grid=(pairs, seqs),
            in_specs=[vec, block, block, block, block, block, pl.BlockSpec((1, 1, heads, seq_len), lambda p, s, n: (p, s, 0, 0))],
            out_specs=[block, block, block, vec],
            scratch_shapes=[pltpu.VMEM((bands, heads * TILE), jnp.float32), pltpu.VMEM((bands, heads * TILE), jnp.float32),
                            pltpu.VMEM((seq_len, 128), jnp.float32), pltpu.VMEM((seq_len, 128), jnp.float32)]),
        out_shape=[jax.ShapeDtypeStruct(q.shape, jnp.bfloat16)] * 3 + [jax.ShapeDtypeStruct((pairs, heads, strip), jnp.float32)],
        compiler_params=pltpu.CompilerParams(vmem_limit_bytes=56 << 20),
        cost_estimate=pl.CostEstimate(flops=10 * seqs * width * seq_len * seq_len, bytes_accessed=16 * seqs * seq_len * width, transcendentals=0),
        name="unattend",
    )(lengths, tvec, q, k, v, o, do, lse)


def bucket_edges():
    distance = np.arange(1, 512)
    scaled = 8 + np.floor(np.log(distance / 8.0) / np.log(16.0) * 8.0)
    level = np.where(distance < 8, distance, np.minimum(15, scaled))
    return np.array([distance[level >= target][0] for target in range(1, 16)], np.int32)

def levels_of(offset):
    level = jnp.sum((jnp.abs(offset)[:, None] >= jnp.asarray(bucket_edges())).astype(jnp.int32), axis=1)
    return level + 16 * (offset > 0).astype(jnp.int32)

def bias_vectors(table, seq_len, tile=TILE):
    x = jnp.arange(2 * seq_len, dtype=jnp.int32)
    far = seq_len - tile
    offset = jnp.where(x < 2 * seq_len - tile, x - far, x - far - 2 * seq_len)
    onehot = (levels_of(offset)[:, None] == jnp.arange(table.shape[0])).astype(jnp.float32)
    return jnp.einsum("xb,bh->hx", onehot, table.astype(jnp.float32) * LOG2E, precision=lax.Precision.HIGHEST)

def table_sums(diag, buckets, seq_len):
    x = jnp.arange(2 * seq_len, dtype=jnp.int32)
    far = seq_len - TILE
    offset = jnp.where(x < 2 * seq_len - TILE, x - far, x - far - 2 * seq_len)
    onehot = ((levels_of(offset)[:, None] == jnp.arange(buckets)) & (jnp.abs(offset) < seq_len)[:, None]).astype(jnp.float32)
    return jnp.einsum("zb,hz->bh", onehot, diag, precision=lax.Precision.HIGHEST)


def inverse_root(v):
    return lax.rsqrt(jnp.mean(v * v, axis=-1, keepdims=True) + EPS)


def norm_back(v, c, gain, e):
    scaled = e * v * c
    down = c * gain * e - v * (c * c) * jnp.mean(gain * scaled, axis=-1, keepdims=True)
    return down, jnp.sum(scaled, axis=0)


def gelu_pair(u):
    square = u * u
    t = jnp.tanh(GELU * u * (1.0 + CUBIC * square))
    value = 0.5 * u * (1.0 + t)
    slope = 0.5 * (1.0 + t) + 0.5 * u * (1.0 - t * t) * (GELU * (1.0 + 3.0 * CUBIC * square))
    return value, slope


def matmul(a, b, ca=1, cb=0):
    return dot(a, b, ca, cb)


def gather_rows(shard):
    n = lax.axis_size("ctx")
    part = shard.shape[0] // n
    mine = lax.dynamic_slice_in_dim(shard, lax.axis_index("ctx") * part, part, 0)
    return lax.all_gather(mine, ("fsdp", "ctx"), axis=0, tiled=True)


def swap(x):
    return lax.ppermute(x, "ctx", [(0, 1), (1, 0)])


def scatter_rows(grad):
    part = lax.psum_scatter(grad, ("fsdp", "ctx"), scatter_dimension=0, tiled=True)
    if lax.axis_size("ctx") != 2:
        return lax.all_gather(part, "ctx", axis=0, tiled=True).astype(jnp.float32)
    other = swap(part)
    first = lax.axis_index("ctx") == 0
    return jnp.concatenate([jnp.where(first, part, other), jnp.where(first, other, part)], axis=0).astype(jnp.float32)


def to_heads(x):
    if lax.axis_size("ctx") != 2:
        return lax.all_to_all(x, "ctx", split_axis=2, concat_axis=1, tiled=True)
    c = lax.axis_index("ctx")
    width = x.shape[2] // 2
    kept = lax.dynamic_slice_in_dim(x, c * width, width, 2)
    came = swap(lax.dynamic_slice_in_dim(x, (1 - c) * width, width, 2))
    return jnp.concatenate([jnp.where(c == 0, kept, came), jnp.where(c == 0, came, kept)], axis=1)


def to_positions(x):
    if lax.axis_size("ctx") != 2:
        return lax.all_to_all(x, "ctx", split_axis=1, concat_axis=2, tiled=True)
    c = lax.axis_index("ctx")
    width = x.shape[1] // 2
    kept = lax.dynamic_slice_in_dim(x, c * width, width, 1)
    came = swap(lax.dynamic_slice_in_dim(x, (1 - c) * width, width, 1))
    return jnp.concatenate([jnp.where(c == 0, kept, came), jnp.where(c == 0, came, kept)], axis=2)


def per_device(tokens, cotangent, lengths, norm_gain, query_weight, key_weight, value_weight, output_weight,
               ffn_gain, inner_weight, outer_weight, bias_table):
    seqs, block, width = tokens.shape
    rows = seqs * block
    n_ctx = lax.axis_size("ctx")
    n_fsdp = lax.axis_size("fsdp")
    c = lax.axis_index("ctx")
    seq_len = block * n_ctx
    heads = bias_table.shape[1]
    buckets = bias_table.shape[0] * n_fsdp
    shard = query_weight.shape[0]
    own_heads = heads // n_ctx
    pairs = own_heads * HEAD_DIM // 128
    per_pair = 128 // HEAD_DIM
    small = bias_table.size
    low = jnp.bfloat16

    side = jnp.concatenate([norm_gain[:, None], ffn_gain[:, None], jnp.broadcast_to(bias_table.reshape(1, small), (shard, small)),
                            jnp.zeros((shard, 126 - small), low)], axis=1)
    first = gather_rows(jnp.concatenate([query_weight, key_weight, value_weight, side], axis=1))
    w_qkv = first[:, : 3 * width]
    gain_one = first[:, 3 * width].astype(jnp.float32)[None, :]
    gain_two = first[:, 3 * width + 1].astype(jnp.float32)[None, :]
    table = first[::shard, 3 * width + 2 : 3 * width + 2 + small].reshape(buckets, heads)
    second = gather_rows(jnp.concatenate([output_weight, inner_weight], axis=1))
    w_output = second[:, :width]
    w_inner = second[:, width:]
    w_outer = gather_rows(outer_weight)

    own_table = lax.dynamic_slice_in_dim(table, c * own_heads, own_heads, 1)
    vector_q = bias_vectors(own_table, seq_len, QT).reshape(pairs, per_pair, 2 * seq_len)
    vector_k = bias_vectors(own_table, seq_len, TILE).reshape(pairs, per_pair, 2 * seq_len)

    x = tokens.astype(jnp.float32).reshape(rows, width)
    root_one = inverse_root(x)
    normed = (x * root_one * gain_one).astype(low)
    scale = jnp.concatenate([jnp.ones((1, width)), jnp.full((1, width), LOG2E), jnp.ones((1, width))], axis=1)
    qkv = (matmul(normed, w_qkv) * scale).astype(low).reshape(seqs, block, 3 * width)
    q, k, v = (to_heads(qkv[:, :, i * width : (i + 1) * width]) for i in range(3))
    out, lse = attend(lengths, vector_q, q, k, v, HEAD_DIM)
    mixed = to_positions(out).reshape(rows, width)
    residual = x + matmul(mixed, w_output)
    root_two = inverse_root(residual)
    normed_ffn = (residual * root_two * gain_two).astype(low)
    hidden, slope = gelu_pair(matmul(normed_ffn, w_inner))
    hidden = hidden.astype(low)
    slope = slope.astype(low)
    layer_out = (residual + matmul(hidden, w_outer)).astype(low).reshape(seqs, block, width)

    position = c * block + jnp.arange(block, dtype=jnp.int32)
    live = (position[None, :] < lengths[:, None])[:, :, None]
    grad_out = jnp.where(live, cotangent, 0).reshape(rows, width)
    outer_grad = matmul(hidden, grad_out, 0, 0).astype(low)
    grad_inner = (matmul(grad_out, w_outer, 1, 1) * slope.astype(jnp.float32)).astype(low)
    inner_grad = matmul(normed_ffn, grad_inner, 0, 0).astype(low)
    down, ffn_gain_grad = norm_back(residual, root_two, gain_two, matmul(grad_inner, w_inner, 1, 1))
    grad_residual = grad_out.astype(jnp.float32) + down
    grad_residual_low = grad_residual.astype(low)
    output_grad = matmul(mixed, grad_residual_low, 0, 0).astype(low)
    grad_mixed = matmul(grad_residual_low, w_output, 1, 1).astype(low).reshape(seqs, block, width)
    grad_mixed = to_heads(grad_mixed)
    dq, dk, dv, diagonals = unattend(lengths, vector_k, q, k, v, out, grad_mixed, lse, HEAD_DIM)
    grads = jnp.concatenate([to_positions(g) for g in (dq, dk, dv)], axis=2).reshape(rows, 3 * width)
    qkv_grad = matmul(normed, grads, 0, 0).astype(low)
    down, norm_gain_grad = norm_back(x, root_one, gain_one, matmul(grads, w_qkv, 1, 1))
    token_grad = (grad_residual + down).reshape(seqs, block, width)

    own_sums = table_sums(diagonals.reshape(own_heads, 2 * seq_len), buckets, seq_len)
    sums = lax.dynamic_update_slice_in_dim(jnp.zeros((buckets, heads), jnp.float32), own_sums, c * own_heads, 1)
    sums = jnp.zeros((n_fsdp, shard, small), jnp.float32).at[:, 0, :].set(sums.reshape(n_fsdp, small)).reshape(n_fsdp * shard, small)
    side = jnp.concatenate([norm_gain_grad[:, None], ffn_gain_grad[:, None], sums, jnp.zeros((n_fsdp * shard, 126 - small), jnp.float32)], axis=1).astype(low)

    outer_grad = scatter_rows(outer_grad)
    second = scatter_rows(jnp.concatenate([output_grad, inner_grad], axis=1))
    first = scatter_rows(jnp.concatenate([qkv_grad, side], axis=1))
    table_grad = first[0, 3 * width + 2 : 3 * width + 2 + small].reshape(bias_table.shape)
    return (layer_out, token_grad, first[:, 3 * width], first[:, :width], first[:, width : 2 * width], first[:, 2 * width : 3 * width],
            second[:, :width], first[:, 3 * width + 1], second[:, width:], outer_grad, table_grad)


def solution(mesh):
    rows = P("fsdp", "ctx", None)
    in_specs = (rows, rows, P("fsdp"), P("fsdp"), P("fsdp", None), P("fsdp", None), P("fsdp", None), P("fsdp", None),
                P("fsdp"), P("fsdp", None), P("fsdp", None), P("fsdp", None))
    out_specs = (rows, rows, P("fsdp"), P("fsdp", None), P("fsdp", None), P("fsdp", None), P("fsdp", None),
                 P("fsdp"), P("fsdp", None), P("fsdp", None), P("fsdp", None))
    return jax.shard_map(per_device, mesh=mesh, in_specs=in_specs, out_specs=out_specs, check_vma=False)
```

```python
import functools

import jax
import jax.numpy as jnp
import numpy as np
from jax import lax
from jax.experimental import pallas as pl
from jax.experimental.pallas import tpu as pltpu
from jax.sharding import PartitionSpec as P

LOG2E = 1.4426950408889634
LN2 = 0.6931471805599453
NEG = -1e30
TILE = 256
QT = 512
HEAD_DIM = 64
EPS = 1e-6
GELU = 0.7978845608028654
CUBIC = 0.044715
VMEM_LIMIT = 60 << 20
CHIPS = (4, 2, 2)
PIECE = 1664


def dot(a, b, ca, cb, precision=None):
    return lax.dot_general(a, b, (((ca,), (cb,)), ((), ())), precision=precision, preferred_element_type=jnp.float32)


def offsets(c, parts, block):
    return [pl.ds(pl.multiple_of(lax.rem(c + parts - j, parts) * block, block), block) for j in range(parts)]


def attend_kernel(info_ref, tvec_ref, *refs, seq_len, head_dim, parts):
    pieces, outs = refs[:parts], refs[parts : 2 * parts]
    lse_ref, strip_ref, q_ref, k_ref, v_ref, o_ref = refs[2 * parts :]
    places = offsets(info_ref[0], parts, seq_len // parts)
    for j in range(parts):
        for t, ref in enumerate((q_ref, k_ref, v_ref)):
            ref[places[j], :] = pieces[j][t, 0]

    heads = q_ref.shape[-1] // head_dim
    blocks = seq_len // TILE
    far = seq_len - QT

    @pl.when(pl.program_id(1) == 0)
    def _():
        for h in range(heads):
            wide = jnp.broadcast_to(tvec_ref[0, h : h + 1, :], (QT, tvec_ref.shape[-1]))
            strip_ref[h] = pltpu.roll(wide, 0, 1, stride=1, stride_axis=0)

    live = info_ref[1 + pl.program_id(1)]
    lane = lax.broadcasted_iota(jnp.int32, (1, q_ref.shape[-1]), 1) // head_dim
    column = lax.broadcasted_iota(jnp.int32, (1, TILE), 1)

    def with_blocks(used):
        top = TILE * used
        kept = [lane == h for h in range(heads)]
        keys = [jnp.where(kept[h], k_ref[0:top, :], 0) for h in range(heads)]
        values = [jnp.where(kept[h], v_ref[0:top, :], 1) for h in range(heads)]

        def query_tile(a, carry):
            here = pl.ds(pl.multiple_of(a * QT, QT), QT)
            q = q_ref[here, :]
            total = None
            for h in range(heads):
                at = pl.ds(pl.multiple_of(far - QT * a, TILE), top)
                scores = dot(q, keys[h], 1, 1) + strip_ref[h, :, at]
                last = jnp.where(column + (top - TILE) < live, scores[:, top - TILE :], NEG)
                scores = jnp.concatenate([scores[:, : top - TILE], last], axis=1) if used > 1 else last
                peak = jnp.max(scores, axis=1, keepdims=True)
                probs = jnp.exp2(scores - peak).astype(jnp.bfloat16)
                out = dot(probs, values[h], 1, 0)
                mass = pltpu.roll(out, head_dim, 1)
                out = out * (1.0 / mass)
                total = out if total is None else jnp.where(kept[h], out, total)
                lse = peak + jnp.log2(mass)
                lse_ref[0, 0, h : h + 1, here] = jnp.transpose(lse)[h * head_dim : h * head_dim + 1, :]
            o_ref[here, :] = total.astype(jnp.bfloat16)
            return carry

        lax.fori_loop(0, seq_len // QT, query_tile, 0, unroll=True)

    for used in range(1, blocks + 1):
        pl.when((live + TILE - 1) // TILE == used)(functools.partial(with_blocks, used))

    for j in range(parts):
        outs[j][0] = o_ref[places[j], :]


def attend(info, tvec, pieces, head_dim):
    parts = len(pieces)
    _, seqs, block, width = pieces[0].shape
    seq_len = block * parts
    pairs = width // 128
    heads = 128 // head_dim
    strip = tvec.shape[-1]
    three = pl.BlockSpec((3, 1, block, 128), lambda p, s, n: (0, s, 0, p))
    one = pl.BlockSpec((1, block, 128), lambda p, s, n: (s, 0, p))
    return pl.pallas_call(
        functools.partial(attend_kernel, seq_len=seq_len, head_dim=head_dim, parts=parts),
        grid_spec=pltpu.PrefetchScalarGridSpec(
            num_scalar_prefetch=1, grid=(pairs, seqs),
            in_specs=[pl.BlockSpec((1, heads, strip), lambda p, s, n: (p, 0, 0))] + [three] * parts,
            out_specs=[one] * parts + [pl.BlockSpec((1, 1, heads, seq_len), lambda p, s, n: (p, s, 0, 0))],
            scratch_shapes=[pltpu.VMEM((heads, QT, strip), jnp.float32)] + [pltpu.VMEM((seq_len, 128), jnp.bfloat16)] * 4),
        out_shape=[jax.ShapeDtypeStruct((seqs, block, width), jnp.bfloat16)] * parts + [jax.ShapeDtypeStruct((pairs, seqs, heads, seq_len), jnp.float32)],
        compiler_params=pltpu.CompilerParams(vmem_limit_bytes=VMEM_LIMIT),
        cost_estimate=pl.CostEstimate(flops=16 * seqs * width * seq_len * seq_len, bytes_accessed=8 * seqs * seq_len * width, transcendentals=0),
        name="attend",
    )(info, tvec, *pieces)


def unattend_kernel(info_ref, tvec_ref, *refs, seq_len, head_dim, parts):
    pieces, out_pieces, do_pieces = refs[:parts], refs[parts : 2 * parts], refs[2 * parts : 3 * parts]
    lse_ref = refs[3 * parts]
    grads, dt_ref = refs[3 * parts + 1 : 4 * parts + 1], refs[4 * parts + 1]
    strip_ref, sums_ref, dk_acc, dv_acc, q_ref, k_ref, v_ref, o_ref, do_ref, dq_ref = refs[4 * parts + 2 :]
    places = offsets(info_ref[0], parts, seq_len // parts)
    for j in range(parts):
        for t, ref in enumerate((q_ref, k_ref, v_ref)):
            ref[places[j], :] = pieces[j][t, 0]
        o_ref[places[j], :] = out_pieces[j][0]
        do_ref[places[j], :] = do_pieces[j][0]
    heads = q_ref.shape[-1] // head_dim
    blocks = seq_len // TILE
    far = seq_len - TILE
    bands = (2 * blocks - 1) * TILE

    @pl.when(pl.program_id(1) == 0)
    def _():
        for h in range(heads):
            wide = jnp.broadcast_to(tvec_ref[0, h : h + 1, :], (TILE, tvec_ref.shape[-1]))
            wide = pltpu.roll(wide, 0, 1, stride=1, stride_axis=0)
            for b in range(2 * blocks - 1):
                strip_ref[TILE * b : TILE * (b + 1), TILE * h : TILE * (h + 1)] = jnp.transpose(wide[:, TILE * b : TILE * (b + 1)])
        sums_ref[...] = jnp.zeros_like(sums_ref)

    live = info_ref[1 + pl.program_id(1)]
    lane = lax.broadcasted_iota(jnp.int32, (1, q_ref.shape[-1]), 1) // head_dim
    row = lax.broadcasted_iota(jnp.int32, (TILE, 1), 0)
    kept = [lane == h for h in range(heads)]

    def with_blocks(used):
        top = TILE * used
        dk_acc[0:top, :] = jnp.zeros((top, dk_acc.shape[1]), jnp.float32)
        dv_acc[0:top, :] = jnp.zeros((top, dv_acc.shape[1]), jnp.float32)

        def query_tile(a, carry):
            here = pl.ds(pl.multiple_of(a * TILE, TILE), TILE)
            q = q_ref[here, :]
            do = do_ref[here, :]
            product = jnp.transpose(do.astype(jnp.float32) * o_ref[here, :].astype(jnp.float32))
            qs = jnp.concatenate([jnp.where(kept[h], q, 0) for h in range(heads)], axis=0)
            dos = jnp.concatenate([jnp.where(kept[h], do, 0) for h in range(heads)], axis=0)
            delta = jnp.concatenate([jnp.sum(product[h * head_dim : (h + 1) * head_dim], axis=0, keepdims=True) for h in range(heads)], axis=1)
            lse = jnp.concatenate([lse_ref[0, 0, h : h + 1, here] for h in range(heads)], axis=1)
            at = pl.ds(pl.multiple_of(far - TILE * a, TILE), top)
            kb = k_ref[0:top, :]
            vb = v_ref[0:top, :]
            p = jnp.exp2(dot(kb, qs, 1, 1) + strip_ref[at, :] - lse)
            last = jnp.where(row + (top - TILE) < live, p[top - TILE :], 0.0)
            p = jnp.concatenate([p[: top - TILE], last], axis=0) if used > 1 else last
            ds = p * (dot(vb, dos, 1, 1) - delta)
            sums_ref[at, :] += ds
            p = p.astype(jnp.bfloat16)
            ds = ds.astype(jnp.bfloat16)
            dv_acc[0:top, :] += dot(p, dos, 1, 0)
            dk_acc[0:top, :] += dot(ds, qs, 1, 0)
            dq = dot(ds, kb, 0, 0)
            dq_total = dq[0:TILE]
            for h in range(1, heads):
                dq_total = jnp.where(kept[h], dq[TILE * h : TILE * (h + 1)], dq_total)
            dq_ref[here, :] = (dq_total * LN2).astype(jnp.bfloat16)
            return carry

        lax.fori_loop(0, used, query_tile, 0)
        if used < blocks:
            dq_ref[top:, :] = jnp.zeros((seq_len - top, q_ref.shape[-1]), jnp.bfloat16)
            dk_acc[top:, :] = jnp.zeros((seq_len - top, q_ref.shape[-1]), jnp.float32)
            dv_acc[top:, :] = jnp.zeros((seq_len - top, q_ref.shape[-1]), jnp.float32)

    for used in range(1, blocks + 1):
        pl.when((live + TILE - 1) // TILE == used)(functools.partial(with_blocks, used))

    for j in range(parts):
        grads[j][0, 0] = dq_ref[places[j], :]
        grads[j][1, 0] = dk_acc[places[j], :].astype(jnp.bfloat16)
        grads[j][2, 0] = dv_acc[places[j], :].astype(jnp.bfloat16)

    @pl.when(pl.program_id(1) == pl.num_programs(1) - 1)
    def _():
        wide = dt_ref.shape[-1]
        for h in range(heads):
            turned = jnp.concatenate([jnp.transpose(sums_ref[TILE * b : TILE * (b + 1), TILE * h : TILE * (h + 1)]) for b in range(2 * blocks - 1)]
                                     + [jnp.zeros((TILE, wide - bands), jnp.float32)], axis=1)
            group = turned[0:8]
            for g in range(1, TILE // 8):
                group = group + pltpu.roll(turned[8 * g : 8 * (g + 1)], wide - 8 * g, 1)
            diagonal = group[0:1]
            for s in range(1, 8):
                diagonal = diagonal + pltpu.roll(group[s : s + 1], wide - s, 1)
            dt_ref[0, h : h + 1, :] = diagonal


def unattend(info, tvec, pieces, outs, do, lse, head_dim):
    parts = len(pieces)
    _, seqs, block, width = pieces[0].shape
    seq_len = block * parts
    pairs = width // 128
    heads = 128 // head_dim
    strip = tvec.shape[-1]
    bands = 2 * seq_len - TILE
    three = pl.BlockSpec((3, 1, block, 128), lambda p, s, n: (0, s, 0, p))
    one = pl.BlockSpec((1, block, 128), lambda p, s, n: (s, 0, p))
    vec = pl.BlockSpec((1, heads, strip), lambda p, s, n: (p, 0, 0))
    return pl.pallas_call(
        functools.partial(unattend_kernel, seq_len=seq_len, head_dim=head_dim, parts=parts),
        grid_spec=pltpu.PrefetchScalarGridSpec(
            num_scalar_prefetch=1, grid=(pairs, seqs),
            in_specs=[vec] + [three] * parts + [one] * (2 * parts) + [pl.BlockSpec((1, 1, heads, seq_len), lambda p, s, n: (p, s, 0, 0))],
            out_specs=[three] * parts + [vec],
            scratch_shapes=[pltpu.VMEM((bands, heads * TILE), jnp.float32), pltpu.VMEM((bands, heads * TILE), jnp.float32),
                            pltpu.VMEM((seq_len, 128), jnp.float32), pltpu.VMEM((seq_len, 128), jnp.float32)]
            + [pltpu.VMEM((seq_len, 128), jnp.bfloat16)] * 6),
        out_shape=[jax.ShapeDtypeStruct((3, seqs, block, width), jnp.bfloat16)] * parts + [jax.ShapeDtypeStruct((pairs, heads, strip), jnp.float32)],
        compiler_params=pltpu.CompilerParams(vmem_limit_bytes=VMEM_LIMIT),
        cost_estimate=pl.CostEstimate(flops=40 * seqs * width * seq_len * seq_len, bytes_accessed=16 * seqs * seq_len * width, transcendentals=0),
        name="unattend",
    )(info, tvec, *pieces, *outs, *do, lse)


def bucket_edges():
    distance = np.arange(1, 512)
    scaled = 8 + np.floor(np.log(distance / 8.0) / np.log(16.0) * 8.0)
    level = np.where(distance < 8, distance, np.minimum(15, scaled))
    return np.array([distance[level >= target][0] for target in range(1, 16)], np.int32)

def levels_of(offset):
    level = jnp.sum((jnp.abs(offset)[:, None] >= jnp.asarray(bucket_edges())).astype(jnp.int32), axis=1)
    return level + 16 * (offset > 0).astype(jnp.int32)

def bias_vectors(table, seq_len, tile=TILE):
    x = jnp.arange(2 * seq_len, dtype=jnp.int32)
    far = seq_len - tile
    offset = jnp.where(x < 2 * seq_len - tile, x - far, x - far - 2 * seq_len)
    onehot = (levels_of(offset)[:, None] == jnp.arange(table.shape[0])).astype(jnp.float32)
    return jnp.einsum("xb,bh->hx", onehot, table.astype(jnp.float32) * LOG2E, precision=lax.Precision.HIGHEST)

def table_sums(diag, buckets, seq_len):
    x = jnp.arange(2 * seq_len, dtype=jnp.int32)
    far = seq_len - TILE
    offset = jnp.where(x < 2 * seq_len - TILE, x - far, x - far - 2 * seq_len)
    onehot = ((levels_of(offset)[:, None] == jnp.arange(buckets)) & (jnp.abs(offset) < seq_len)[:, None]).astype(jnp.float32)
    return jnp.einsum("zb,hz->bh", onehot, diag, precision=lax.Precision.HIGHEST)


class Place:
    def __init__(self):
        c = lax.axis_index("ctx")
        f = lax.axis_index("fsdp")
        self.c = c
        self.other = 1 - c
        z, y, x = f // 4, (f // 2) % 2, f % 2
        self.z, self.up, self.down, self.far = z, (z + 1) % 4, (z + 3) % 4, (z + 2) % 4
        self.own = (y, x)
        self.u = ((y + c) % 2, (x + 1 - c) % 2)
        self.w = ((y + 1 - c) % 2, (x + c) % 2)
        self.uw = (1 - y, 1 - x)
        flat = lambda zz, col: {"fsdp": zz * 4 + col[0] * 2 + col[1]}
        self.to = {"u": flat(z, self.u), "w": flat(z, self.w), "up": flat(self.up, self.own),
                   "down": flat(self.down, self.own), "core": {"ctx": 1 - c}}

    def greet(self):
        barrier = pltpu.get_barrier_semaphore()
        for target in self.to.values():
            pl.semaphore_signal(barrier, inc=1, device_id=target, device_id_type=pl.DeviceIdType.MESH)
        pl.semaphore_wait(barrier, len(self.to))


class Copies:
    def __init__(self, place, send, recv):
        self.place, self.send, self.recv = place, send, recv
        self.made = {}

    def start(self, name, src, dst, to):
        i = len(self.made)
        copy = pltpu.make_async_remote_copy(src_ref=src, dst_ref=dst, send_sem=self.send.at[i], recv_sem=self.recv.at[i],
                                            device_id=self.place.to[to], device_id_type=pl.DeviceIdType.MESH)
        copy.start()
        self.made[name] = copy

    def arrived(self, name):
        self.made[name].wait_recv()

    def finish(self):
        for copy in self.made.values():
            copy.wait_send()


def windows(columns, size):
    cuts = list(range(0, columns, size))
    if len(cuts) > 1 and columns - cuts[-1] < size // 2:
        cuts.pop()
    return [(a, b - a) for a, b in zip(cuts, cuts[1:] + [columns])]


def gather_steps(i, shard, out, window, place, copies, local):
    p = place
    columns = pl.ds(*window)
    name = lambda s: (i, s)
    levels = [p.z, p.down, p.far, p.up]
    at = lambda k, col: out.at[levels[k], col[0], col[1], p.c, :, columns]
    mine = shard.at[p.c, :, columns]
    theirs = shard.at[p.other, :, columns]
    kept = [pltpu.make_async_copy(mine, at(0, p.own), local.at[2 * i]),
            pltpu.make_async_copy(theirs, out.at[p.z, p.own[0], p.own[1], p.other, :, columns], local.at[2 * i + 1])]

    def own(k):
        if k == 0:
            for copy in kept:
                copy.start()
        else:
            copies.arrived(name("z %d" % k))
        source = mine if k == 0 else at(k, p.own)
        if k < 3:
            copies.start(name("z %d" % (k + 1)), source, at(k, p.own), "up")
        copies.start(name("u %d" % k), source, at(k, p.own), "u")
        copies.start(name("w own %d" % k), source, at(k, p.own), "w")
        if k > 0:
            copies.start(name("core own %d" % k), source, at(k, p.own), "core")

    def turn(k):
        copies.arrived(name("u %d" % k))
        copies.start(name("w u %d" % k), at(k, p.u), at(k, p.u), "w")
        copies.start(name("core u %d" % k), at(k, p.u), at(k, p.u), "core")

    def across(k):
        copies.arrived(name("w own %d" % k))
        copies.start(name("core w %d" % k), at(k, p.w), at(k, p.w), "core")
        copies.arrived(name("w u %d" % k))
        copies.start(name("core uw %d" % k), at(k, p.uw), at(k, p.uw), "core")

    def end():
        for k in range(4):
            for what in ("own", "u", "w", "uw"):
                if k > 0 or what != "own":
                    copies.arrived(name("core %s %d" % (what, k)))
        for copy in kept:
            copy.wait()

    def step(n):
        if n < 4:
            own(n)
        if 0 <= n - 1 < 4:
            turn(n - 1)
        if 0 <= n - 2 < 4:
            across(n - 2)

    return [functools.partial(step, n) for n in range(6)] + [end]


GATHER_COPIES = 3 + 4 + 8 + 15


def staggered(chains):
    for step in range(len(chains) - 1 + max(len(chain) for chain in chains)):
        for i, chain in enumerate(chains):
            if 0 <= step - i < len(chain):
                chain[step - i]()


def gather_kernel(*refs, count):
    shards, outs = refs[:count], refs[count : 2 * count]
    send, recv, local = refs[2 * count :]
    place = Place()
    place.greet()
    copies = Copies(place, send, recv)
    parts = [(i, window) for i in range(count) for window in windows(shards[i].shape[-1], PIECE)]
    staggered([gather_steps(n, shards[i], outs[i], window, place, copies, local) for n, (i, window) in enumerate(parts)])
    copies.finish()


def gather_all(shards, collective_id):
    split = [s.reshape(2, s.shape[0] // 2, s.shape[1]) for s in shards]
    count = len(shards)
    parts = sum(len(windows(s.shape[-1], PIECE)) for s in split)
    anywhere = pl.BlockSpec(memory_space=pl.ANY)
    outs = pl.pallas_call(
        functools.partial(gather_kernel, count=count),
        in_specs=[anywhere] * count,
        out_specs=[anywhere] * count,
        out_shape=[jax.ShapeDtypeStruct(CHIPS + s.shape, s.dtype) for s in split],
        scratch_shapes=[pltpu.SemaphoreType.DMA((GATHER_COPIES * parts,)), pltpu.SemaphoreType.DMA((GATHER_COPIES * parts,)),
                        pltpu.SemaphoreType.DMA((2 * parts,))],
        compiler_params=pltpu.CompilerParams(collective_id=collective_id, has_side_effects=True),
        name="gather_rows",
    )(*split)
    return [o.reshape(-1, o.shape[-1]) for o in outs]


def add_into(acc, came):
    lead = acc.shape[:-2]
    total = int(np.prod(lead))
    if total == 1:
        index = (0,) * len(lead)
        acc[index] = acc[index] + came[index]
        return

    def body(n, carry):
        index = []
        for extent in reversed(lead):
            index.append(n % extent)
            n = n // extent
        index = tuple(reversed(index))
        acc[index] = acc[index] + came[index]
        return carry

    lax.fori_loop(0, total, body, 0)


def scatter_buffers(rows, columns):
    shapes = [(4, 2, 2), (4, 2, 2), (2, 4), (4,), (3,)]
    return [pltpu.VMEM(lead + (rows, columns), jnp.bfloat16) for lead in shapes]


SCATTER_BUFFERS = 5
SCATTER_COPIES = 1 + 2 + 1 + 3 + 1


def scatter_steps(i, grad, out, window, buffers, place, copies, local):
    p = place
    acc, came, by_w, by_u, by_z = buffers
    columns = pl.ds(*window)
    name = lambda s: (i, s)
    line = lambda col: acc.at[:, col[0], col[1]]
    at = lambda z: acc.at[z, p.own[0], p.own[1]]
    load = pltpu.make_async_copy(grad.at[:, :, :, p.c, :, columns], acc, local.at[i])

    def first():
        load.start()
        copies.start(name("core"), grad.at[:, :, :, p.other, :, columns], came, "core")

    def second():
        load.wait()
        copies.arrived(name("core"))
        add_into(line(p.uw), came.at[:, p.uw[0], p.uw[1]])
        copies.start(name("w 1"), line(p.uw), by_w.at[1], "w")
        add_into(line(p.w), came.at[:, p.w[0], p.w[1]])
        copies.start(name("w 0"), line(p.w), by_w.at[0], "w")
        add_into(line(p.u), came.at[:, p.u[0], p.u[1]])
        add_into(line(p.own), came.at[:, p.own[0], p.own[1]])

    def third():
        copies.arrived(name("w 1"))
        add_into(line(p.u), by_w.at[1])
        copies.start(name("u"), line(p.u), by_u, "u")
        copies.arrived(name("w 0"))
        add_into(line(p.own), by_w.at[0])

    def fourth():
        copies.arrived(name("u"))
        add_into(line(p.own), by_u)
        copies.start(name("z 0"), at(p.down), by_z.at[0], "up")

    def climb(k, level):
        def run():
            copies.arrived(name("z %d" % k))
            add_into(at(level), by_z.at[k])
            copies.start(name("z %d" % (k + 1)), at(level), by_z.at[k + 1], "up")
        return run

    def last():
        copies.arrived(name("z 2"))
        out[p.c, :, columns] = at(p.z)[...] + by_z[2]
        copies.start(name("out"), out.at[p.c, :, columns], out.at[p.c, :, columns], "core")

    def end():
        copies.arrived(name("out"))

    return [first, second, third, fourth, climb(0, p.far), climb(1, p.up), last, end]


def scatter_kernel(*refs, count):
    grads, outs = refs[:count], refs[count : 2 * count]
    parts = [(i, window) for i in range(count) for window in windows(grads[i].shape[-1], PIECE)]
    buffers = [refs[2 * count + SCATTER_BUFFERS * n : 2 * count + SCATTER_BUFFERS * (n + 1)] for n in range(len(parts))]
    send, recv, local = refs[2 * count + SCATTER_BUFFERS * len(parts) :]
    place = Place()
    place.greet()
    copies = Copies(place, send, recv)
    staggered([scatter_steps(n, grads[i], outs[i], window, buffers[n], place, copies, local) for n, (i, window) in enumerate(parts)])
    copies.finish()


def scatter_all(grads, collective_id):
    split = [g.reshape(CHIPS + (2, g.shape[0] // 32, g.shape[1])) for g in grads]
    count = len(grads)
    parts = [(g.shape[-2], window[1]) for g in split for window in windows(g.shape[-1], PIECE)]
    outs = pl.pallas_call(
        functools.partial(scatter_kernel, count=count),
        in_specs=[pl.BlockSpec(memory_space=pl.ANY)] * count,
        out_specs=[pl.BlockSpec(memory_space=pltpu.VMEM)] * count,
        out_shape=[jax.ShapeDtypeStruct(g.shape[3:], g.dtype) for g in split],
        scratch_shapes=[b for part in parts for b in scatter_buffers(*part)]
        + [pltpu.SemaphoreType.DMA((SCATTER_COPIES * len(parts),)), pltpu.SemaphoreType.DMA((SCATTER_COPIES * len(parts),)),
           pltpu.SemaphoreType.DMA((len(parts),))],
        compiler_params=pltpu.CompilerParams(collective_id=collective_id, has_side_effects=True, vmem_limit_bytes=60 << 20),
        name="scatter_rows",
    )(*split)
    return [o.reshape(-1, o.shape[-1]) for o in outs]


def inverse_root(v):
    return lax.rsqrt(jnp.mean(v * v, axis=-1, keepdims=True) + EPS)


def norm_back(v, c, gain, e):
    scaled = e * v * c
    down = c * gain * e - v * (c * c) * jnp.mean(gain * scaled, axis=-1, keepdims=True)
    return down, jnp.sum(scaled, axis=0, keepdims=True)


def gelu_pair(u):
    square = u * u
    t = jnp.tanh(u * (GELU + GELU * CUBIC * square))
    half = 0.5 * u
    slope = 0.5 + 0.5 * t + half * (1.0 - t * t) * (GELU + 3.0 * GELU * CUBIC * square)
    return half + half * t, slope


def group(c, j, parts):
    return lax.rem(c + j, parts)


def resident(shape):
    return pl.BlockSpec(shape, lambda i, n: (0,) * len(shape), pipeline_mode=pl.Buffered(1))


def tiles(shape, axis):
    at = lambda i, n: tuple(i if a == axis else 0 for a in range(len(shape)))
    return pl.BlockSpec(shape, at)


def params():
    return pltpu.CompilerParams(vmem_limit_bytes=VMEM_LIMIT)


def cost(flops, size):
    return pl.CostEstimate(flops=int(flops), bytes_accessed=int(size), transcendentals=0)


def project_kernel(info_ref, x_ref, gain_ref, w_ref, normed_ref, *outs, parts):
    c = info_ref[0]
    x = x_ref[...].astype(jnp.float32)
    width = x.shape[1]
    share = width // parts
    normed = (x * inverse_root(x) * gain_ref[...]).astype(jnp.bfloat16)
    normed_ref[...] = normed
    for j in reversed(range(parts)):
        for t in range(3):
            at = pl.ds(pl.multiple_of(t * width + group(c, j, parts) * share, 128), share)
            y = dot(normed, w_ref[:, at], 1, 0)
            outs[j][t] = (y * LOG2E if t == 1 else y).astype(jnp.bfloat16)


def project(info, x, gain, w, parts):
    rows, width = x.shape
    tile = min(512, rows)
    share = width // parts
    return pl.pallas_call(
        functools.partial(project_kernel, parts=parts),
        grid_spec=pltpu.PrefetchScalarGridSpec(
            num_scalar_prefetch=1, grid=(rows // tile,),
            in_specs=[tiles((tile, width), 0), resident((1, width)), resident(w.shape)],
            out_specs=[tiles((tile, width), 0)] + [tiles((3, tile, share), 1)] * parts),
        out_shape=[jax.ShapeDtypeStruct((rows, width), jnp.bfloat16)] + [jax.ShapeDtypeStruct((3, rows, share), jnp.bfloat16)] * parts,
        compiler_params=params(),
        cost_estimate=cost(6 * rows * width * width, 10 * rows * width + 6 * width * width),
        name="project",
    )(info, x, gain, w)


def feed_kernel(info_ref, x_ref, cot_ref, gain_ref, wo_ref, w_ref, *refs, parts, block):
    mixed = refs[:parts]
    mixed_ref, normed_ref, hidden_ref, layer_ref, inner_ref, residual_ref, low_ref, gain_grad_ref = refs[parts : parts + 8]
    grads = refs[parts + 8 : 2 * parts + 8]
    slope_ref = refs[2 * parts + 8]
    c = info_ref[0]
    tile, width = x_ref.shape
    share = width // parts
    chunk = w_ref.shape[0]
    hidden_width = w_ref.shape[1] // 2
    low = jnp.bfloat16
    rows_of = [pl.ds(pl.multiple_of(group(c, j, parts) * share, 128), share) for j in range(parts)]

    residual = x_ref[...].astype(jnp.float32)
    for j in range(parts):
        mixed_ref[:, rows_of[j]] = mixed[j][...]
        residual = residual + dot(mixed[j][...], wo_ref[rows_of[j], :], 1, 0)
    root = inverse_root(residual)
    gain = gain_ref[...]
    normed = (residual * root * gain).astype(low)
    normed_ref[...] = normed
    layer = None
    for k in range(0, hidden_width, chunk):
        value, slope = gelu_pair(dot(normed, w_ref[:, k : k + chunk], 1, 0))
        value = value.astype(low)
        hidden_ref[:, k : k + chunk] = value
        slope_ref[:, k : k + chunk] = slope.astype(slope_ref.dtype)
        part = dot(value, w_ref[:, hidden_width + k : hidden_width + k + chunk], 1, 0)
        layer = part if layer is None else layer + part
    layer_ref[...] = (residual + layer).astype(low)

    start = pl.program_id(0) * tile
    position = c * block + lax.rem(start, block) + lax.broadcasted_iota(jnp.int32, (tile, 1), 0)
    grad = jnp.where(position < info_ref[1 + start // block], cot_ref[...], 0)
    up = None
    for k in range(0, hidden_width, chunk):
        inner = (dot(grad, w_ref[:, hidden_width + k : hidden_width + k + chunk], 1, 1) * slope_ref[:, k : k + chunk].astype(jnp.float32)).astype(low)
        inner_ref[:, k : k + chunk] = inner
        part = dot(inner, w_ref[:, k : k + chunk], 1, 1)
        up = part if up is None else up + part
    down, gain_grad = norm_back(residual, root, gain, up)

    @pl.when(pl.program_id(0) == 0)
    def _():
        gain_grad_ref[...] = jnp.zeros_like(gain_grad_ref)

    gain_grad_ref[...] += gain_grad
    down = down + grad.astype(jnp.float32)
    residual_ref[...] = down
    down = down.astype(low)
    low_ref[...] = down
    for j in range(parts):
        grads[j][...] = dot(down, wo_ref[rows_of[j], :], 1, 1).astype(low)


def feed(info, x, cot, gain, wo, w, mixed, block, tile=256):
    parts = len(mixed)
    rows, width = x.shape
    hidden = w.shape[1] // 2
    tile = min(tile, block)
    share = width // parts
    t = lambda w: tiles((tile, w), 0)
    low = lambda w: jax.ShapeDtypeStruct((rows, w), jnp.bfloat16)
    return pl.pallas_call(
        functools.partial(feed_kernel, parts=parts, block=block),
        grid_spec=pltpu.PrefetchScalarGridSpec(
            num_scalar_prefetch=1, grid=(rows // tile,),
            in_specs=[t(width), t(width), resident((1, width)), resident(wo.shape), resident(w.shape)] + [t(share)] * parts,
            out_specs=[t(width), t(width), t(hidden), t(width), t(hidden), t(width), t(width), resident((1, width))] + [t(share)] * parts,
            scratch_shapes=[pltpu.VMEM((tile, hidden), jnp.bfloat16)]),
        out_shape=[low(width), low(width), low(hidden), low(width), low(hidden), jax.ShapeDtypeStruct((rows, width), jnp.float32), low(width),
                   jax.ShapeDtypeStruct((1, width), jnp.float32)] + [low(share)] * parts,
        compiler_params=params(),
        cost_estimate=cost(rows * width * (8 * hidden + 4 * width), rows * (18 * width + 4 * hidden) + 4 * width * hidden),
        name="feed",
    )(info, x, cot, gain, wo, w, *mixed)


def unproject_kernel(info_ref, x_ref, residual_ref, gain_ref, w_ref, *refs, parts):
    came = refs[:parts]
    token_ref, grads_ref, gain_grad_ref = refs[parts:]
    c = info_ref[0]
    x = x_ref[...].astype(jnp.float32)
    width = x.shape[1]
    share = width // parts
    up = None
    for j in range(parts):
        for t in range(3):
            at = pl.ds(pl.multiple_of(t * width + group(c, j, parts) * share, 128), share)
            piece = came[j][t]
            grads_ref[:, at] = piece
            part = dot(piece, w_ref[:, at], 1, 1)
            up = part if up is None else up + part
    down, gain_grad = norm_back(x, inverse_root(x), gain_ref[...], up)

    @pl.when(pl.program_id(0) == 0)
    def _():
        gain_grad_ref[...] = jnp.zeros_like(gain_grad_ref)

    gain_grad_ref[...] += gain_grad
    token_ref[...] = residual_ref[...] + down


def unproject(info, x, residual, gain, w, came):
    parts = len(came)
    rows, width = x.shape
    tile = min(512, rows)
    share = width // parts
    return pl.pallas_call(
        functools.partial(unproject_kernel, parts=parts),
        grid_spec=pltpu.PrefetchScalarGridSpec(
            num_scalar_prefetch=1, grid=(rows // tile,),
            in_specs=[tiles((tile, width), 0), tiles((tile, width), 0), resident((1, width)), resident(w.shape)] + [tiles((3, tile, share), 1)] * parts,
            out_specs=[tiles((tile, width), 0), tiles((tile, 3 * width), 0), resident((1, width))]),
        out_shape=[jax.ShapeDtypeStruct((rows, width), jnp.float32), jax.ShapeDtypeStruct((rows, 3 * width), jnp.bfloat16), jax.ShapeDtypeStruct((1, width), jnp.float32)],
        compiler_params=params(),
        cost_estimate=cost(6 * rows * width * width, 22 * rows * width + 6 * width * width),
        name="unproject",
    )(info, x, residual, gain, w, *came)


def gather_rows(shard):
    n = lax.axis_size("ctx")
    part = shard.shape[0] // n
    mine = lax.dynamic_slice_in_dim(shard, lax.axis_index("ctx") * part, part, 0)
    return lax.all_gather(mine, ("fsdp", "ctx"), axis=0, tiled=True)


def scatter_rows(grad):
    part = lax.psum_scatter(grad, ("fsdp", "ctx"), scatter_dimension=0, tiled=True)
    if lax.axis_size("ctx") != 2:
        return lax.all_gather(part, "ctx", axis=0, tiled=True)
    other = lax.ppermute(part, "ctx", [(0, 1), (1, 0)])
    first = lax.axis_index("ctx") == 0
    return jnp.concatenate([jnp.where(first, part, other), jnp.where(first, other, part)], axis=0)


def exchange(pieces):
    n = len(pieces)
    return [pieces[0]] + [lax.ppermute(pieces[j], "ctx", [(i, (i + j) % n) for i in range(n)]) for j in range(1, n)]


def give_back(pieces):
    n = len(pieces)
    return [pieces[0]] + [lax.ppermute(pieces[j], "ctx", [(i, (i - j) % n) for i in range(n)]) for j in range(1, n)]


def by_chip(shape):
    return shape == (2, 16)


def per_device(tokens, cotangent, lengths, norm_gain, query_weight, key_weight, value_weight, output_weight,
               ffn_gain, inner_weight, outer_weight, bias_table):
    seqs, block, width = tokens.shape
    rows = seqs * block
    n_ctx = lax.axis_size("ctx")
    n_fsdp = lax.axis_size("fsdp")
    c = lax.axis_index("ctx")
    seq_len = block * n_ctx
    heads = bias_table.shape[1]
    buckets = bias_table.shape[0] * n_fsdp
    shard = query_weight.shape[0]
    hidden_width = inner_weight.shape[1]
    slabs = hidden_width // width
    own_heads = heads // n_ctx
    pairs = own_heads * HEAD_DIM // 128
    per_pair = 128 // HEAD_DIM
    small = bias_table.size
    share = width // n_ctx
    low = jnp.bfloat16
    remote = by_chip((n_ctx, n_fsdp))
    info = jnp.concatenate([jnp.full((1,), c, jnp.int32), lengths])

    inner = inner_weight.reshape(shard, n_fsdp, slabs, shard).transpose(0, 2, 1, 3).reshape(shard, hidden_width)
    outer = outer_weight.reshape(slabs, shard, width).transpose(1, 0, 2).reshape(shard, slabs * width)
    w_feed = gather_rows(jnp.concatenate([inner, outer], axis=1))
    side = jnp.concatenate([norm_gain[:, None], ffn_gain[:, None], jnp.broadcast_to(bias_table.reshape(1, small), (shard, small)),
                            jnp.zeros((shard, 126 - small), low)], axis=1)
    first = jnp.concatenate([query_weight, key_weight, value_weight, side], axis=1)
    if remote:
        first, w_output = gather_all([first, output_weight], 1)
    else:
        first, w_output = gather_rows(first), gather_rows(output_weight)
    side = first[:, 3 * width :]
    gain_one = side[:, 0].astype(jnp.float32)[None, :]
    gain_two = side[:, 1].astype(jnp.float32)[None, :]
    table = side[::shard, 2 : 2 + small].reshape(buckets, heads)
    own_table = lax.dynamic_slice_in_dim(table, c * own_heads, own_heads, 1)
    vector_q = bias_vectors(own_table, seq_len, QT).reshape(pairs, per_pair, 2 * seq_len)
    vector_k = bias_vectors(own_table, seq_len, TILE).reshape(pairs, per_pair, 2 * seq_len)

    x = tokens.reshape(rows, width)
    cot = cotangent.reshape(rows, width)
    normed, *qkv = project(info, x, gain_one, first, n_ctx)
    qkv = exchange([p.reshape(3, seqs, block, share) for p in qkv])
    *out, lse = attend(info, vector_q, qkv, HEAD_DIM)
    mixed = [m.reshape(rows, share) for m in give_back(out)]
    (mixed, normed_ffn, hidden, layer_out, grad_inner, grad_residual, grad_low, ffn_gain_grad, *grad_mixed) = feed(
        info, x, cot, gain_two, w_output, w_feed, mixed, block)
    grad_mixed = exchange([g.reshape(seqs, block, share) for g in grad_mixed])

    position = c * block + jnp.arange(block, dtype=jnp.int32)
    live = (position[None, :] < lengths[:, None])[:, :, None]
    grad_out = jnp.where(live, cotangent, 0).reshape(rows, width)
    inner_grad = dot(normed_ffn, grad_inner, 0, 0).astype(low)
    outer_grad = [dot(hidden[:, q * width : (q + 1) * width], grad_out, 0, 0).astype(low) for q in range(slabs)]
    feed_grad = jnp.concatenate([inner_grad] + outer_grad, axis=1)
    feed_grad, grad_mixed = lax.optimization_barrier((feed_grad, grad_mixed))
    feed_grad = scatter_rows(feed_grad)

    *grads, diagonals = unattend(info, vector_k, qkv, out, grad_mixed, lse, HEAD_DIM)
    grads = [g.reshape(3, rows, share) for g in give_back(grads)]
    token_grad, grads, norm_gain_grad = unproject(info, x, grad_residual, gain_one, first, grads)
    output_grad = dot(mixed, grad_low, 0, 0).astype(low)
    qkv_grad = dot(normed, grads, 0, 0).astype(low)

    own_sums = table_sums(diagonals.reshape(own_heads, 2 * seq_len), buckets, seq_len)
    sums = lax.dynamic_update_slice_in_dim(jnp.zeros((buckets, heads), jnp.float32), own_sums, c * own_heads, 1)
    sums = jnp.zeros((n_fsdp, shard, small), jnp.float32).at[:, 0, :].set(sums.reshape(n_fsdp, small)).reshape(n_fsdp * shard, small)
    side = jnp.concatenate([norm_gain_grad.reshape(-1, 1), ffn_gain_grad.reshape(-1, 1), sums, jnp.zeros((n_fsdp * shard, 126 - small), jnp.float32)], axis=1)
    second = jnp.concatenate([output_grad, side.astype(low)], axis=1)
    if remote:
        second, qkv_grad = scatter_all([second, qkv_grad], 2)
    else:
        second, qkv_grad = scatter_rows(second), scatter_rows(qkv_grad)

    full = jnp.float32
    second = second.astype(full)
    qkv_grad = qkv_grad.astype(full)
    feed_grad = feed_grad.astype(full)
    inner_grad = feed_grad[:, :hidden_width].reshape(shard, slabs, n_fsdp, shard).transpose(0, 2, 1, 3).reshape(shard, hidden_width)
    outer_grad = feed_grad[:, hidden_width:].reshape(shard, slabs, width).transpose(1, 0, 2).reshape(slabs * shard, width)
    table_grad = second[0, width + 2 : width + 2 + small].reshape(bias_table.shape)
    return (layer_out.reshape(tokens.shape), token_grad.reshape(tokens.shape), second[:, width], qkv_grad[:, :width], qkv_grad[:, width : 2 * width],
            qkv_grad[:, 2 * width :], second[:, :width], second[:, width + 1], inner_grad, outer_grad, table_grad)


def solution(mesh):
    rows = P("fsdp", "ctx", None)
    in_specs = (rows, rows, P("fsdp"), P("fsdp"), P("fsdp", None), P("fsdp", None), P("fsdp", None), P("fsdp", None),
                P("fsdp"), P("fsdp", None), P("fsdp", None), P("fsdp", None))
    out_specs = (rows, rows, P("fsdp"), P("fsdp", None), P("fsdp", None), P("fsdp", None), P("fsdp", None),
                 P("fsdp"), P("fsdp", None), P("fsdp", None), P("fsdp", None))
    return jax.shard_map(per_device, mesh=mesh, in_specs=in_specs, out_specs=out_specs, check_vma=False)
```

```python
import functools

import jax
import jax.numpy as jnp
import numpy as np
from jax import lax
from jax.experimental import pallas as pl
from jax.experimental.pallas import tpu as pltpu
from jax.sharding import PartitionSpec as P

LOG2E = 1.4426950408889634
LN2 = 0.6931471805599453
NEG = -1e30
TILE = 256
QT = 256
HEAD_DIM = 64
EPS = 1e-6
GELU = 0.7978845608028654
CUBIC = 0.044715
VMEM_LIMIT = 60 << 20
CHIPS = (4, 2, 2)
PIECE = 1664


def dot(a, b, ca, cb, precision=None):
    return lax.dot_general(a, b, (((ca,), (cb,)), ((), ())), precision=precision, preferred_element_type=jnp.float32)


def offsets(c, parts, block):
    return [pl.ds(pl.multiple_of(lax.rem(c + parts - j, parts) * block, block), block) for j in range(parts)]


def attend_kernel(info_ref, tvec_ref, *refs, seq_len, head_dim, parts):
    pieces, outs = refs[:parts], refs[parts : 2 * parts]
    lse_ref, strip_ref, q_ref, k_ref, v_ref, o_ref = refs[2 * parts :]
    places = offsets(info_ref[0], parts, seq_len // parts)
    for j in range(parts):
        for t, ref in enumerate((q_ref, k_ref, v_ref)):
            ref[places[j], :] = pieces[j][t, 0]

    heads = q_ref.shape[-1] // head_dim
    blocks = seq_len // TILE
    far = seq_len - QT

    @pl.when(pl.program_id(1) == 0)
    def _():
        for h in range(heads):
            wide = jnp.broadcast_to(tvec_ref[0, h : h + 1, :], (QT, tvec_ref.shape[-1]))
            strip_ref[h] = pltpu.roll(wide, 0, 1, stride=1, stride_axis=0)

    live = info_ref[1 + pl.program_id(1)]
    lane = lax.broadcasted_iota(jnp.int32, (1, q_ref.shape[-1]), 1) // head_dim
    column = lax.broadcasted_iota(jnp.int32, (1, TILE), 1)

    def with_blocks(used):
        top = TILE * used
        kept = [lane == h for h in range(heads)]
        keys = [jnp.where(kept[h], k_ref[0:top, :], 0) for h in range(heads)]
        ones = jnp.ones((top, 128), jnp.bfloat16)
        values = [jnp.concatenate([jnp.where(kept[h], v_ref[0:top, :], 0), ones], axis=1) for h in range(heads)]

        def query_tile(a, carry):
            here = pl.ds(pl.multiple_of(a * QT, QT), QT)
            q = q_ref[here, :]
            total = None
            for h in range(heads):
                at = pl.ds(pl.multiple_of(far - QT * a, TILE), top)
                scores = dot(q, keys[h], 1, 1) + strip_ref[h, :, at]
                last = jnp.where(column + (top - TILE) < live, scores[:, top - TILE :], NEG)
                scores = jnp.concatenate([scores[:, : top - TILE], last], axis=1) if used > 1 else last
                peak = jnp.max(scores, axis=1, keepdims=True)
                probs = jnp.exp2(scores - peak).astype(jnp.bfloat16)
                out = dot(probs, values[h], 1, 0)
                mass = out[:, 128:]
                out = out[:, :128] * (1.0 / mass)
                total = out if total is None else total + out
                lse = peak + jnp.log2(mass)
                both = lse if h == 0 else jnp.where(kept[h], lse, both)
            both = jnp.transpose(both)
            for h in range(heads):
                lse_ref[0, 0, h : h + 1, here] = both[h * head_dim : h * head_dim + 1, :]
            o_ref[here, :] = total.astype(jnp.bfloat16)
            return carry

        lax.fori_loop(0, seq_len // QT, query_tile, 0, unroll=True)

    for used in range(1, blocks + 1):
        pl.when((live + TILE - 1) // TILE == used)(functools.partial(with_blocks, used))

    for j in range(parts):
        outs[j][0] = o_ref[places[j], :]


def attend(info, tvec, pieces, head_dim):
    parts = len(pieces)
    _, seqs, block, width = pieces[0].shape
    seq_len = block * parts
    pairs = width // 128
    heads = 128 // head_dim
    strip = tvec.shape[-1]
    three = pl.BlockSpec((3, 1, block, 128), lambda p, s, n: (0, s, 0, p))
    one = pl.BlockSpec((1, block, 128), lambda p, s, n: (s, 0, p))
    return pl.pallas_call(
        functools.partial(attend_kernel, seq_len=seq_len, head_dim=head_dim, parts=parts),
        grid_spec=pltpu.PrefetchScalarGridSpec(
            num_scalar_prefetch=1, grid=(pairs, seqs),
            in_specs=[pl.BlockSpec((1, heads, strip), lambda p, s, n: (p, 0, 0))] + [three] * parts,
            out_specs=[one] * parts + [pl.BlockSpec((1, 1, heads, seq_len), lambda p, s, n: (p, s, 0, 0))],
            scratch_shapes=[pltpu.VMEM((heads, QT, strip), jnp.float32)] + [pltpu.VMEM((seq_len, 128), jnp.bfloat16)] * 4),
        out_shape=[jax.ShapeDtypeStruct((seqs, block, width), jnp.bfloat16)] * parts + [jax.ShapeDtypeStruct((pairs, seqs, heads, seq_len), jnp.float32)],
        compiler_params=pltpu.CompilerParams(vmem_limit_bytes=VMEM_LIMIT),
        cost_estimate=pl.CostEstimate(flops=16 * seqs * width * seq_len * seq_len, bytes_accessed=8 * seqs * seq_len * width, transcendentals=0),
        name="attend",
    )(info, tvec, *pieces)


def unattend_kernel(info_ref, tvec_ref, *refs, seq_len, head_dim, parts):
    pieces, out_pieces, do_pieces = refs[:parts], refs[parts : 2 * parts], refs[2 * parts : 3 * parts]
    lse_ref = refs[3 * parts]
    grads, dt_ref = refs[3 * parts + 1 : 4 * parts + 1], refs[4 * parts + 1]
    strip_ref, sums_ref, dk_acc, dv_acc, q_ref, k_ref, v_ref, o_ref, do_ref, dq_ref = refs[4 * parts + 2 :]
    places = offsets(info_ref[0], parts, seq_len // parts)
    for j in range(parts):
        for t, ref in enumerate((q_ref, k_ref, v_ref)):
            ref[places[j], :] = pieces[j][t, 0]
        o_ref[places[j], :] = out_pieces[j][0]
        do_ref[places[j], :] = do_pieces[j][0]
    heads = q_ref.shape[-1] // head_dim
    blocks = seq_len // TILE
    far = seq_len - TILE
    bands = (2 * blocks - 1) * TILE

    @pl.when(pl.program_id(1) == 0)
    def _():
        for h in range(heads):
            wide = jnp.broadcast_to(tvec_ref[0, h : h + 1, :], (TILE, tvec_ref.shape[-1]))
            wide = pltpu.roll(wide, 0, 1, stride=1, stride_axis=0)
            for b in range(2 * blocks - 1):
                strip_ref[TILE * b : TILE * (b + 1), TILE * h : TILE * (h + 1)] = jnp.transpose(wide[:, TILE * b : TILE * (b + 1)])
        sums_ref[...] = jnp.zeros_like(sums_ref)

    live = info_ref[1 + pl.program_id(1)]
    lane = lax.broadcasted_iota(jnp.int32, (1, q_ref.shape[-1]), 1) // head_dim
    row = lax.broadcasted_iota(jnp.int32, (TILE, 1), 0)
    kept = [lane == h for h in range(heads)]

    def with_blocks(used):
        top = TILE * used
        dk_acc[0:top, :] = jnp.zeros((top, dk_acc.shape[1]), jnp.float32)
        dv_acc[0:top, :] = jnp.zeros((top, dv_acc.shape[1]), jnp.float32)

        def query_tile(a, carry):
            here = pl.ds(pl.multiple_of(a * TILE, TILE), TILE)
            q = q_ref[here, :]
            do = do_ref[here, :]
            product = jnp.transpose(do.astype(jnp.float32) * o_ref[here, :].astype(jnp.float32))
            qs = jnp.concatenate([jnp.where(kept[h], q, 0) for h in range(heads)], axis=0)
            dos = jnp.concatenate([jnp.where(kept[h], do, 0) for h in range(heads)], axis=0)
            delta = jnp.concatenate([jnp.sum(product[h * head_dim : (h + 1) * head_dim], axis=0, keepdims=True) for h in range(heads)], axis=1)
            lse = jnp.concatenate([lse_ref[0, 0, h : h + 1, here] for h in range(heads)], axis=1)
            at = pl.ds(pl.multiple_of(far - TILE * a, TILE), top)
            kb = k_ref[0:top, :]
            vb = v_ref[0:top, :]
            p = jnp.exp2(dot(kb, qs, 1, 1) + strip_ref[at, :] - lse)
            last = jnp.where(row + (top - TILE) < live, p[top - TILE :], 0.0)
            p = jnp.concatenate([p[: top - TILE], last], axis=0) if used > 1 else last
            ds = p * (dot(vb, dos, 1, 1) - delta)
            sums_ref[at, :] += ds
            p = p.astype(jnp.bfloat16)
            ds = ds.astype(jnp.bfloat16)
            dv_acc[0:top, :] += dot(p, dos, 1, 0)
            dk_acc[0:top, :] += dot(ds, qs, 1, 0)
            dq = dot(ds, kb, 0, 0)
            dq_total = dq[0:TILE]
            for h in range(1, heads):
                dq_total = jnp.where(kept[h], dq[TILE * h : TILE * (h + 1)], dq_total)
            dq_ref[here, :] = (dq_total * LN2).astype(jnp.bfloat16)
            return carry

        lax.fori_loop(0, used, query_tile, 0, unroll=2)
        if used < blocks:
            dq_ref[top:, :] = jnp.zeros((seq_len - top, q_ref.shape[-1]), jnp.bfloat16)
            dk_acc[top:, :] = jnp.zeros((seq_len - top, q_ref.shape[-1]), jnp.float32)
            dv_acc[top:, :] = jnp.zeros((seq_len - top, q_ref.shape[-1]), jnp.float32)

    for used in range(1, blocks + 1):
        pl.when((live + TILE - 1) // TILE == used)(functools.partial(with_blocks, used))

    for j in range(parts):
        grads[j][0, 0] = dq_ref[places[j], :]
        grads[j][1, 0] = dk_acc[places[j], :].astype(jnp.bfloat16)
        grads[j][2, 0] = dv_acc[places[j], :].astype(jnp.bfloat16)

    @pl.when(pl.program_id(1) == pl.num_programs(1) - 1)
    def _():
        wide = dt_ref.shape[-1]
        for h in range(heads):
            turned = jnp.concatenate([jnp.transpose(sums_ref[TILE * b : TILE * (b + 1), TILE * h : TILE * (h + 1)]) for b in range(2 * blocks - 1)]
                                     + [jnp.zeros((TILE, wide - bands), jnp.float32)], axis=1)
            group = turned[0:8]
            for g in range(1, TILE // 8):
                group = group + pltpu.roll(turned[8 * g : 8 * (g + 1)], wide - 8 * g, 1)
            diagonal = group[0:1]
            for s in range(1, 8):
                diagonal = diagonal + pltpu.roll(group[s : s + 1], wide - s, 1)
            dt_ref[0, h : h + 1, :] = diagonal


def unattend(info, tvec, pieces, outs, do, lse, head_dim):
    parts = len(pieces)
    _, seqs, block, width = pieces[0].shape
    seq_len = block * parts
    pairs = width // 128
    heads = 128 // head_dim
    strip = tvec.shape[-1]
    bands = 2 * seq_len - TILE
    three = pl.BlockSpec((3, 1, block, 128), lambda p, s, n: (0, s, 0, p))
    one = pl.BlockSpec((1, block, 128), lambda p, s, n: (s, 0, p))
    vec = pl.BlockSpec((1, heads, strip), lambda p, s, n: (p, 0, 0))
    return pl.pallas_call(
        functools.partial(unattend_kernel, seq_len=seq_len, head_dim=head_dim, parts=parts),
        grid_spec=pltpu.PrefetchScalarGridSpec(
            num_scalar_prefetch=1, grid=(pairs, seqs),
            in_specs=[vec] + [three] * parts + [one] * (2 * parts) + [pl.BlockSpec((1, 1, heads, seq_len), lambda p, s, n: (p, s, 0, 0))],
            out_specs=[three] * parts + [vec],
            scratch_shapes=[pltpu.VMEM((bands, heads * TILE), jnp.float32), pltpu.VMEM((bands, heads * TILE), jnp.float32),
                            pltpu.VMEM((seq_len, 128), jnp.float32), pltpu.VMEM((seq_len, 128), jnp.float32)]
            + [pltpu.VMEM((seq_len, 128), jnp.bfloat16)] * 6),
        out_shape=[jax.ShapeDtypeStruct((3, seqs, block, width), jnp.bfloat16)] * parts + [jax.ShapeDtypeStruct((pairs, heads, strip), jnp.float32)],
        compiler_params=pltpu.CompilerParams(vmem_limit_bytes=VMEM_LIMIT),
        cost_estimate=pl.CostEstimate(flops=40 * seqs * width * seq_len * seq_len, bytes_accessed=16 * seqs * seq_len * width, transcendentals=0),
        name="unattend",
    )(info, tvec, *pieces, *outs, *do, lse)


def bucket_edges():
    distance = np.arange(1, 512)
    scaled = 8 + np.floor(np.log(distance / 8.0) / np.log(16.0) * 8.0)
    level = np.where(distance < 8, distance, np.minimum(15, scaled))
    return np.array([distance[level >= target][0] for target in range(1, 16)], np.int32)

def levels_of(offset):
    level = jnp.sum((jnp.abs(offset)[:, None] >= jnp.asarray(bucket_edges())).astype(jnp.int32), axis=1)
    return level + 16 * (offset > 0).astype(jnp.int32)

def bias_vectors(table, seq_len, tile=TILE):
    x = jnp.arange(2 * seq_len, dtype=jnp.int32)
    far = seq_len - tile
    offset = jnp.where(x < 2 * seq_len - tile, x - far, x - far - 2 * seq_len)
    onehot = (levels_of(offset)[:, None] == jnp.arange(table.shape[0])).astype(jnp.float32)
    return jnp.einsum("xb,bh->hx", onehot, table.astype(jnp.float32) * LOG2E, precision=lax.Precision.HIGHEST)

def table_sums(diag, buckets, seq_len):
    x = jnp.arange(2 * seq_len, dtype=jnp.int32)
    far = seq_len - TILE
    offset = jnp.where(x < 2 * seq_len - TILE, x - far, x - far - 2 * seq_len)
    onehot = ((levels_of(offset)[:, None] == jnp.arange(buckets)) & (jnp.abs(offset) < seq_len)[:, None]).astype(jnp.float32)
    return jnp.einsum("zb,hz->bh", onehot, diag, precision=lax.Precision.HIGHEST)


class Place:
    def __init__(self):
        c = lax.axis_index("ctx")
        f = lax.axis_index("fsdp")
        self.c = c
        self.other = 1 - c
        z, y, x = f // 4, (f // 2) % 2, f % 2
        self.z, self.up, self.down, self.far = z, (z + 1) % 4, (z + 3) % 4, (z + 2) % 4
        self.own = (y, x)
        self.u = ((y + c) % 2, (x + 1 - c) % 2)
        self.w = ((y + 1 - c) % 2, (x + c) % 2)
        self.uw = (1 - y, 1 - x)
        flat = lambda zz, col: {"fsdp": zz * 4 + col[0] * 2 + col[1]}
        self.to = {"u": flat(z, self.u), "w": flat(z, self.w), "up": flat(self.up, self.own),
                   "down": flat(self.down, self.own), "core": {"ctx": 1 - c}}

    def greet(self):
        barrier = pltpu.get_barrier_semaphore()
        for target in self.to.values():
            pl.semaphore_signal(barrier, inc=1, device_id=target, device_id_type=pl.DeviceIdType.MESH)
        pl.semaphore_wait(barrier, len(self.to))


class Copies:
    def __init__(self, place, send, recv):
        self.place, self.send, self.recv = place, send, recv
        self.made = {}

    def start(self, name, src, dst, to):
        i = len(self.made)
        copy = pltpu.make_async_remote_copy(src_ref=src, dst_ref=dst, send_sem=self.send.at[i], recv_sem=self.recv.at[i],
                                            device_id=self.place.to[to], device_id_type=pl.DeviceIdType.MESH)
        copy.start()
        self.made[name] = copy

    def arrived(self, name):
        self.made[name].wait_recv()

    def finish(self):
        for copy in self.made.values():
            copy.wait_send()


def windows(columns, size):
    cuts = list(range(0, columns, size))
    if len(cuts) > 1 and columns - cuts[-1] < size // 2:
        cuts.pop()
    return [(a, b - a) for a, b in zip(cuts, cuts[1:] + [columns])]


def gather_steps(i, shard, out, window, place, copies, local):
    p = place
    columns = pl.ds(*window)
    name = lambda s: (i, s)
    levels = [p.z, p.down, p.far, p.up]
    at = lambda k, col: out.at[levels[k], col[0], col[1], p.c, :, columns]
    mine = shard.at[p.c, :, columns]
    theirs = shard.at[p.other, :, columns]
    kept = [pltpu.make_async_copy(mine, at(0, p.own), local.at[2 * i]),
            pltpu.make_async_copy(theirs, out.at[p.z, p.own[0], p.own[1], p.other, :, columns], local.at[2 * i + 1])]

    def own(k):
        if k == 0:
            for copy in kept:
                copy.start()
        else:
            copies.arrived(name("z %d" % k))
        source = mine if k == 0 else at(k, p.own)
        if k < 3:
            copies.start(name("z %d" % (k + 1)), source, at(k, p.own), "up")
        copies.start(name("u %d" % k), source, at(k, p.own), "u")
        copies.start(name("w own %d" % k), source, at(k, p.own), "w")
        if k > 0:
            copies.start(name("core own %d" % k), source, at(k, p.own), "core")

    def turn(k):
        copies.arrived(name("u %d" % k))
        copies.start(name("w u %d" % k), at(k, p.u), at(k, p.u), "w")
        copies.start(name("core u %d" % k), at(k, p.u), at(k, p.u), "core")

    def across(k):
        copies.arrived(name("w own %d" % k))
        copies.start(name("core w %d" % k), at(k, p.w), at(k, p.w), "core")
        copies.arrived(name("w u %d" % k))
        copies.start(name("core uw %d" % k), at(k, p.uw), at(k, p.uw), "core")

    def end():
        for k in range(4):
            for what in ("own", "u", "w", "uw"):
                if k > 0 or what != "own":
                    copies.arrived(name("core %s %d" % (what, k)))
        for copy in kept:
            copy.wait()

    def step(n):
        if n < 4:
            own(n)
        if 0 <= n - 1 < 4:
            turn(n - 1)
        if 0 <= n - 2 < 4:
            across(n - 2)

    return [functools.partial(step, n) for n in range(6)] + [end]


GATHER_COPIES = 3 + 4 + 8 + 15


def staggered(chains):
    for step in range(len(chains) - 1 + max(len(chain) for chain in chains)):
        for i, chain in enumerate(chains):
            if 0 <= step - i < len(chain):
                chain[step - i]()


def gather_kernel(*refs, count):
    shards, outs = refs[:count], refs[count : 2 * count]
    send, recv, local = refs[2 * count :]
    place = Place()
    place.greet()
    copies = Copies(place, send, recv)
    parts = [(i, window) for i in range(count) for window in windows(shards[i].shape[-1], PIECE)]
    staggered([gather_steps(n, shards[i], outs[i], window, place, copies, local) for n, (i, window) in enumerate(parts)])
    copies.finish()


def gather_all(shards, collective_id):
    split = [s.reshape(2, s.shape[0] // 2, s.shape[1]) for s in shards]
    count = len(shards)
    parts = sum(len(windows(s.shape[-1], PIECE)) for s in split)
    anywhere = pl.BlockSpec(memory_space=pl.ANY)
    outs = pl.pallas_call(
        functools.partial(gather_kernel, count=count),
        in_specs=[anywhere] * count,
        out_specs=[anywhere] * count,
        out_shape=[jax.ShapeDtypeStruct(CHIPS + s.shape, s.dtype) for s in split],
        scratch_shapes=[pltpu.SemaphoreType.DMA((GATHER_COPIES * parts,)), pltpu.SemaphoreType.DMA((GATHER_COPIES * parts,)),
                        pltpu.SemaphoreType.DMA((2 * parts,))],
        compiler_params=pltpu.CompilerParams(collective_id=collective_id, has_side_effects=True),
        name="gather_rows",
    )(*split)
    return [o.reshape(-1, o.shape[-1]) for o in outs]


def add_into(acc, came):
    lead = acc.shape[:-2]
    total = int(np.prod(lead))
    if total == 1:
        index = (0,) * len(lead)
        acc[index] = acc[index] + came[index]
        return

    def body(n, carry):
        index = []
        for extent in reversed(lead):
            index.append(n % extent)
            n = n // extent
        index = tuple(reversed(index))
        acc[index] = acc[index] + came[index]
        return carry

    lax.fori_loop(0, total, body, 0)


def scatter_buffers(rows, columns):
    shapes = [(4, 2, 2), (4, 2, 2), (2, 4), (4,), (3,)]
    return [pltpu.VMEM(lead + (rows, columns), jnp.bfloat16) for lead in shapes]


SCATTER_BUFFERS = 5
SCATTER_COPIES = 1 + 2 + 1 + 3 + 1


def scatter_steps(i, grad, out, window, buffers, place, copies, local):
    p = place
    acc, came, by_w, by_u, by_z = buffers
    columns = pl.ds(*window)
    name = lambda s: (i, s)
    line = lambda col: acc.at[:, col[0], col[1]]
    at = lambda z: acc.at[z, p.own[0], p.own[1]]
    load = pltpu.make_async_copy(grad.at[:, :, :, p.c, :, columns], acc, local.at[i])

    def first():
        load.start()
        copies.start(name("core"), grad.at[:, :, :, p.other, :, columns], came, "core")

    def second():
        load.wait()
        copies.arrived(name("core"))
        add_into(line(p.uw), came.at[:, p.uw[0], p.uw[1]])
        copies.start(name("w 1"), line(p.uw), by_w.at[1], "w")
        add_into(line(p.w), came.at[:, p.w[0], p.w[1]])
        copies.start(name("w 0"), line(p.w), by_w.at[0], "w")
        add_into(line(p.u), came.at[:, p.u[0], p.u[1]])
        add_into(line(p.own), came.at[:, p.own[0], p.own[1]])

    def third():
        copies.arrived(name("w 1"))
        add_into(line(p.u), by_w.at[1])
        copies.start(name("u"), line(p.u), by_u, "u")
        copies.arrived(name("w 0"))
        add_into(line(p.own), by_w.at[0])

    def fourth():
        copies.arrived(name("u"))
        add_into(line(p.own), by_u)
        copies.start(name("z 0"), at(p.down), by_z.at[0], "up")

    def climb(k, level):
        def run():
            copies.arrived(name("z %d" % k))
            add_into(at(level), by_z.at[k])
            copies.start(name("z %d" % (k + 1)), at(level), by_z.at[k + 1], "up")
        return run

    def last():
        copies.arrived(name("z 2"))
        out[p.c, :, columns] = at(p.z)[...] + by_z[2]
        copies.start(name("out"), out.at[p.c, :, columns], out.at[p.c, :, columns], "core")

    def end():
        copies.arrived(name("out"))

    return [first, second, third, fourth, climb(0, p.far), climb(1, p.up), last, end]


def scatter_kernel(*refs, count):
    grads, outs = refs[:count], refs[count : 2 * count]
    parts = [(i, window) for i in range(count) for window in windows(grads[i].shape[-1], PIECE)]
    buffers = [refs[2 * count + SCATTER_BUFFERS * n : 2 * count + SCATTER_BUFFERS * (n + 1)] for n in range(len(parts))]
    send, recv, local = refs[2 * count + SCATTER_BUFFERS * len(parts) :]
    place = Place()
    place.greet()
    copies = Copies(place, send, recv)
    staggered([scatter_steps(n, grads[i], outs[i], window, buffers[n], place, copies, local) for n, (i, window) in enumerate(parts)])
    copies.finish()


def scatter_all(grads, collective_id):
    split = [g.reshape(CHIPS + (2, g.shape[0] // 32, g.shape[1])) for g in grads]
    count = len(grads)
    parts = [(g.shape[-2], window[1]) for g in split for window in windows(g.shape[-1], PIECE)]
    outs = pl.pallas_call(
        functools.partial(scatter_kernel, count=count),
        in_specs=[pl.BlockSpec(memory_space=pl.ANY)] * count,
        out_specs=[pl.BlockSpec(memory_space=pltpu.VMEM)] * count,
        out_shape=[jax.ShapeDtypeStruct(g.shape[3:], g.dtype) for g in split],
        scratch_shapes=[b for part in parts for b in scatter_buffers(*part)]
        + [pltpu.SemaphoreType.DMA((SCATTER_COPIES * len(parts),)), pltpu.SemaphoreType.DMA((SCATTER_COPIES * len(parts),)),
           pltpu.SemaphoreType.DMA((len(parts),))],
        compiler_params=pltpu.CompilerParams(collective_id=collective_id, has_side_effects=True, vmem_limit_bytes=60 << 20),
        name="scatter_rows",
    )(*split)
    return [o.reshape(-1, o.shape[-1]) for o in outs]


def inverse_root(v):
    return lax.rsqrt(jnp.mean(v * v, axis=-1, keepdims=True) + EPS)


def norm_back(v, c, gain, e):
    scaled = e * v * c
    down = c * gain * e - v * (c * c) * jnp.mean(gain * scaled, axis=-1, keepdims=True)
    return down, jnp.sum(scaled, axis=0, keepdims=True)


def gelu_pair(u):
    square = u * u
    t = jnp.tanh(u * (GELU + GELU * CUBIC * square))
    half = 0.5 * u
    slope = 0.5 + 0.5 * t + half * (1.0 - t * t) * (GELU + 3.0 * GELU * CUBIC * square)
    return half + half * t, slope


def group(c, j, parts):
    return lax.rem(c + j, parts)


def resident(shape):
    return pl.BlockSpec(shape, lambda i, n: (0,) * len(shape), pipeline_mode=pl.Buffered(1))


def tiles(shape, axis):
    at = lambda i, n: tuple(i if a == axis else 0 for a in range(len(shape)))
    return pl.BlockSpec(shape, at)


def params():
    return pltpu.CompilerParams(vmem_limit_bytes=VMEM_LIMIT)


def cost(flops, size):
    return pl.CostEstimate(flops=int(flops), bytes_accessed=int(size), transcendentals=0)


def project_kernel(info_ref, x_ref, gain_ref, w_ref, normed_ref, *outs, parts):
    c = info_ref[0]
    x = x_ref[...].astype(jnp.float32)
    width = x.shape[1]
    share = width // parts
    normed = (x * inverse_root(x) * gain_ref[...]).astype(jnp.bfloat16)
    normed_ref[...] = normed
    for j in reversed(range(parts)):
        for t in range(3):
            at = pl.ds(pl.multiple_of(t * width + group(c, j, parts) * share, 128), share)
            y = dot(normed, w_ref[:, at], 1, 0)
            outs[j][t] = (y * LOG2E if t == 1 else y).astype(jnp.bfloat16)


def project(info, x, gain, w, parts):
    rows, width = x.shape
    tile = min(256, rows)
    share = width // parts
    return pl.pallas_call(
        functools.partial(project_kernel, parts=parts),
        grid_spec=pltpu.PrefetchScalarGridSpec(
            num_scalar_prefetch=1, grid=(rows // tile,),
            in_specs=[tiles((tile, width), 0), resident((1, width)), resident(w.shape)],
            out_specs=[tiles((tile, width), 0)] + [tiles((3, tile, share), 1)] * parts),
        out_shape=[jax.ShapeDtypeStruct((rows, width), jnp.bfloat16)] + [jax.ShapeDtypeStruct((3, rows, share), jnp.bfloat16)] * parts,
        compiler_params=params(),
        cost_estimate=cost(6 * rows * width * width, 10 * rows * width + 6 * width * width),
        name="project",
    )(info, x, gain, w)


def feed_kernel(info_ref, x_ref, cot_ref, gain_ref, wo_ref, w_ref, *refs, parts, block):
    mixed = refs[:parts]
    mixed_ref, normed_ref, hidden_ref, layer_ref, grad_ref, inner_ref, residual_ref, low_ref, gain_grad_ref = refs[parts : parts + 9]
    grads = refs[parts + 9 : 2 * parts + 9]
    slope_ref = refs[2 * parts + 9]
    c = info_ref[0]
    tile, width = x_ref.shape
    share = width // parts
    chunk = w_ref.shape[0]
    hidden_width = w_ref.shape[1] // 2
    low = jnp.bfloat16
    rows_of = [pl.ds(pl.multiple_of(group(c, j, parts) * share, 128), share) for j in range(parts)]

    residual = x_ref[...].astype(jnp.float32)
    for j in range(parts):
        mixed_ref[:, rows_of[j]] = mixed[j][...]
        residual = residual + dot(mixed[j][...], wo_ref[rows_of[j], :], 1, 0)
    root = inverse_root(residual)
    gain = gain_ref[...]
    normed = (residual * root * gain).astype(low)
    normed_ref[...] = normed
    layer = None
    for k in range(0, hidden_width, chunk):
        value, slope = gelu_pair(dot(normed, w_ref[:, k : k + chunk], 1, 0))
        value = value.astype(low)
        hidden_ref[:, k : k + chunk] = value
        slope_ref[:, k : k + chunk] = slope.astype(slope_ref.dtype)
        part = dot(value, w_ref[:, hidden_width + k : hidden_width + k + chunk], 1, 0)
        layer = part if layer is None else layer + part
    layer_ref[...] = (residual + layer).astype(low)

    start = pl.program_id(0) * tile
    position = c * block + lax.rem(start, block) + lax.broadcasted_iota(jnp.int32, (tile, 1), 0)
    grad = jnp.where(position < info_ref[1 + start // block], cot_ref[...], 0)
    grad_ref[...] = grad
    up = None
    for k in range(0, hidden_width, chunk):
        inner = (dot(grad, w_ref[:, hidden_width + k : hidden_width + k + chunk], 1, 1) * slope_ref[:, k : k + chunk].astype(jnp.float32)).astype(low)
        inner_ref[:, k : k + chunk] = inner
        part = dot(inner, w_ref[:, k : k + chunk], 1, 1)
        up = part if up is None else up + part
    down, gain_grad = norm_back(residual, root, gain, up)

    @pl.when(pl.program_id(0) == 0)
    def _():
        gain_grad_ref[...] = jnp.zeros_like(gain_grad_ref)

    gain_grad_ref[...] += gain_grad
    down = down + grad.astype(jnp.float32)
    residual_ref[...] = down
    down = down.astype(low)
    low_ref[...] = down
    for j in range(parts):
        grads[j][...] = dot(down, wo_ref[rows_of[j], :], 1, 1).astype(low)


def feed(info, x, cot, gain, wo, w, mixed, block, tile=256):
    parts = len(mixed)
    rows, width = x.shape
    hidden = w.shape[1] // 2
    tile = min(tile, block)
    share = width // parts
    t = lambda w: tiles((tile, w), 0)
    low = lambda w: jax.ShapeDtypeStruct((rows, w), jnp.bfloat16)
    return pl.pallas_call(
        functools.partial(feed_kernel, parts=parts, block=block),
        grid_spec=pltpu.PrefetchScalarGridSpec(
            num_scalar_prefetch=1, grid=(rows // tile,),
            in_specs=[t(width), t(width), resident((1, width)), resident(wo.shape), resident(w.shape)] + [t(share)] * parts,
            out_specs=[t(width), t(width), t(hidden), t(width), t(width), t(hidden), t(width), t(width), resident((1, width))] + [t(share)] * parts,
            scratch_shapes=[pltpu.VMEM((tile, hidden), jnp.bfloat16)]),
        out_shape=[low(width), low(width), low(hidden), low(width), low(width), low(hidden), jax.ShapeDtypeStruct((rows, width), jnp.float32), low(width),
                   jax.ShapeDtypeStruct((1, width), jnp.float32)] + [low(share)] * parts,
        compiler_params=params(),
        cost_estimate=cost(rows * width * (8 * hidden + 4 * width), rows * (18 * width + 4 * hidden) + 4 * width * hidden),
        name="feed",
    )(info, x, cot, gain, wo, w, *mixed)


def unproject_kernel(info_ref, x_ref, residual_ref, gain_ref, w_ref, *refs, parts):
    came = refs[:parts]
    token_ref, grads_ref, gain_grad_ref = refs[parts:]
    c = info_ref[0]
    x = x_ref[...].astype(jnp.float32)
    width = x.shape[1]
    share = width // parts
    up = None
    for j in range(parts):
        for t in range(3):
            at = pl.ds(pl.multiple_of(t * width + group(c, j, parts) * share, 128), share)
            piece = came[j][t]
            grads_ref[:, at] = piece
            part = dot(piece, w_ref[:, at], 1, 1)
            up = part if up is None else up + part
    down, gain_grad = norm_back(x, inverse_root(x), gain_ref[...], up)

    @pl.when(pl.program_id(0) == 0)
    def _():
        gain_grad_ref[...] = jnp.zeros_like(gain_grad_ref)

    gain_grad_ref[...] += gain_grad
    token_ref[...] = residual_ref[...] + down


def unproject(info, x, residual, gain, w, came):
    parts = len(came)
    rows, width = x.shape
    tile = min(256, rows)
    share = width // parts
    return pl.pallas_call(
        functools.partial(unproject_kernel, parts=parts),
        grid_spec=pltpu.PrefetchScalarGridSpec(
            num_scalar_prefetch=1, grid=(rows // tile,),
            in_specs=[tiles((tile, width), 0), tiles((tile, width), 0), resident((1, width)), resident(w.shape)] + [tiles((3, tile, share), 1)] * parts,
            out_specs=[tiles((tile, width), 0), tiles((tile, 3 * width), 0), resident((1, width))]),
        out_shape=[jax.ShapeDtypeStruct((rows, width), jnp.float32), jax.ShapeDtypeStruct((rows, 3 * width), jnp.bfloat16), jax.ShapeDtypeStruct((1, width), jnp.float32)],
        compiler_params=params(),
        cost_estimate=cost(6 * rows * width * width, 22 * rows * width + 6 * width * width),
        name="unproject",
    )(info, x, residual, gain, w, *came)


def weigh_kernel(mixed_ref, low_ref, normed_ref, grad_ref, inner_ref, hidden_ref, out_ref, made_ref, came_ref, send, recv, *, slabs):
    s = pl.program_id(0)
    c = lax.axis_index("ctx")
    other = {"ctx": 1 - c}
    total = 2 * slabs + 1

    def copy(k):
        return pltpu.make_async_remote_copy(src_ref=made_ref.at[lax.rem(k, 2), :, 1 - c], dst_ref=came_ref.at[k], send_sem=send.at[k], recv_sem=recv.at[k],
                                            device_id=other, device_id_type=pl.DeviceIdType.MESH)

    @pl.when(s == 0)
    def _():
        barrier = pltpu.get_barrier_semaphore()
        pl.semaphore_signal(barrier, inc=1, device_id=other, device_id_type=pl.DeviceIdType.MESH)
        pl.semaphore_wait(barrier, 1)

    def make(left, right):
        slab = dot(left[...], right[...], 0, 0).astype(jnp.bfloat16)
        made_ref[lax.rem(s, 2)] = slab.reshape(made_ref.shape[1:])
        copy(s).start()

    pl.when(s == 0)(lambda: make(mixed_ref, low_ref))
    pl.when((s > 0) & (s <= slabs))(lambda: make(normed_ref, inner_ref))
    pl.when((s > slabs) & (s < total))(lambda: make(hidden_ref, grad_ref))

    @pl.when(s > 0)
    def _():
        earlier = copy(s - 1)
        earlier.wait_recv()
        out_ref[...] = made_ref[lax.rem(s - 1, 2), :, c] + came_ref[s - 1]
        earlier.wait_send()


def weigh(mixed, low, normed, grad, inner, hidden, chips, collective_id):
    rows, width = mixed.shape
    slabs = hidden.shape[1] // width
    total = 2 * slabs + 1
    part = width // chips // 2
    whole = pl.BlockSpec((rows, width), lambda s: (0, 0), pipeline_mode=pl.Buffered(1))
    slab = lambda first: pl.BlockSpec((rows, width), lambda s: (0, jnp.clip(s - first, 0, slabs - 1)))
    return pl.pallas_call(
        functools.partial(weigh_kernel, slabs=slabs),
        grid=(total + 1,),
        in_specs=[whole, whole, whole, whole, slab(1), slab(1 + slabs)],
        out_specs=pl.BlockSpec((chips, part, width), lambda s: (0, 0, jnp.maximum(s - 1, 0))),
        out_shape=jax.ShapeDtypeStruct((chips, part, total * width), jnp.bfloat16),
        scratch_shapes=[pltpu.VMEM((2, chips, 2, part, width), jnp.bfloat16), pltpu.VMEM((total, chips, part, width), jnp.bfloat16),
                        pltpu.SemaphoreType.DMA((total,)), pltpu.SemaphoreType.DMA((total,))],
        compiler_params=pltpu.CompilerParams(collective_id=collective_id, has_side_effects=True, vmem_limit_bytes=VMEM_LIMIT),
        cost_estimate=cost(2 * rows * width * width * total, 2 * rows * width * 13),
        name="weigh",
    )(mixed, low, normed, grad, inner, hidden)


def gather_rows(shard):
    n = lax.axis_size("ctx")
    part = shard.shape[0] // n
    mine = lax.dynamic_slice_in_dim(shard, lax.axis_index("ctx") * part, part, 0)
    return lax.all_gather(mine, ("fsdp", "ctx"), axis=0, tiled=True)


def scatter_rows(grad):
    part = lax.psum_scatter(grad, ("fsdp", "ctx"), scatter_dimension=0, tiled=True)
    return lax.all_gather(part, "ctx", axis=0, tiled=True)


def both_halves(part):
    other = lax.ppermute(part, "ctx", [(0, 1), (1, 0)])
    first = lax.axis_index("ctx") == 0
    return jnp.concatenate([jnp.where(first, part, other), jnp.where(first, other, part)], axis=0)


def exchange(pieces):
    n = len(pieces)
    return [pieces[0]] + [lax.ppermute(pieces[j], "ctx", [(i, (i + j) % n) for i in range(n)]) for j in range(1, n)]


def give_back(pieces):
    n = len(pieces)
    return [pieces[0]] + [lax.ppermute(pieces[j], "ctx", [(i, (i - j) % n) for i in range(n)]) for j in range(1, n)]


def wide(x):
    return jnp.pad(x, [(0, 0)] * (x.ndim - 1) + [(0, 128 - x.shape[-1])])


def by_chip(shape):
    return shape == (2, 16)


def per_device(tokens, cotangent, lengths, norm_gain, query_weight, key_weight, value_weight, output_weight,
               ffn_gain, inner_weight, outer_weight, bias_table):
    seqs, block, width = tokens.shape
    rows = seqs * block
    n_ctx = lax.axis_size("ctx")
    n_fsdp = lax.axis_size("fsdp")
    c = lax.axis_index("ctx")
    seq_len = block * n_ctx
    heads = bias_table.shape[1]
    buckets = bias_table.shape[0] * n_fsdp
    shard = query_weight.shape[0]
    hidden_width = inner_weight.shape[1]
    slabs = hidden_width // width
    own_heads = heads // n_ctx
    pairs = own_heads * HEAD_DIM // 128
    per_pair = 128 // HEAD_DIM
    small = bias_table.size
    share = width // n_ctx
    low = jnp.bfloat16
    remote = by_chip((n_ctx, n_fsdp))
    info = jnp.concatenate([jnp.full((1,), c, jnp.int32), lengths])

    inner = inner_weight.reshape(shard, n_fsdp, slabs, shard).transpose(0, 2, 1, 3).reshape(shard, hidden_width)
    outer = outer_weight.reshape(slabs, shard, width).transpose(1, 0, 2).reshape(shard, slabs * width)
    w_feed = gather_rows(jnp.concatenate([inner, outer], axis=1))
    side = jnp.stack([wide(norm_gain), wide(ffn_gain), wide(bias_table.reshape(small))])
    side = jnp.pad(side, ((0, shard - 3), (0, 0)))
    first = jnp.concatenate([query_weight, key_weight, value_weight, side], axis=1)
    if remote:
        first, w_output = gather_all([first, output_weight], 1)
    else:
        first, w_output = gather_rows(first), gather_rows(output_weight)
    side = first[:, 3 * width :].reshape(n_fsdp, shard, 128)
    gain_one = side[:, 0, :shard].reshape(1, width).astype(jnp.float32)
    gain_two = side[:, 1, :shard].reshape(1, width).astype(jnp.float32)
    table = side[:, 2, :small].reshape(buckets, heads)
    own_table = lax.dynamic_slice_in_dim(table, c * own_heads, own_heads, 1)
    vector_q = bias_vectors(own_table, seq_len, QT).reshape(pairs, per_pair, 2 * seq_len)
    vector_k = bias_vectors(own_table, seq_len, TILE).reshape(pairs, per_pair, 2 * seq_len)

    x = tokens.reshape(rows, width)
    cot = cotangent.reshape(rows, width)
    normed, *qkv = project(info, x, gain_one, first, n_ctx)
    qkv = exchange([p.reshape(3, seqs, block, share) for p in qkv])
    *out, lse = attend(info, vector_q, qkv, HEAD_DIM)
    mixed = [m.reshape(rows, share) for m in give_back(out)]
    (mixed, normed_ffn, hidden, layer_out, grad_out, grad_inner, grad_residual, grad_low, ffn_gain_grad, *grad_mixed) = feed(
        info, x, cot, gain_two, w_output, w_feed, mixed, block)
    grad_mixed = exchange([g.reshape(seqs, block, share) for g in grad_mixed])

    if remote:
        feed_grad = weigh(mixed, grad_low, normed_ffn, grad_out, grad_inner, hidden, n_fsdp, 3)
        feed_grad, grad_mixed = lax.optimization_barrier((feed_grad, grad_mixed))
        feed_grad = lax.psum_scatter(feed_grad, "fsdp", scatter_dimension=0, tiled=False)
        feed_grad = both_halves(feed_grad)
    else:
        outer_grad = [dot(hidden[:, q * width : (q + 1) * width], grad_out, 0, 0) for q in range(slabs)]
        feed_grad = jnp.concatenate([dot(mixed, grad_low, 0, 0), dot(normed_ffn, grad_inner, 0, 0)] + outer_grad, axis=1).astype(low)
        feed_grad = scatter_rows(feed_grad)

    *grads, diagonals = unattend(info, vector_k, qkv, out, grad_mixed, lse, HEAD_DIM)
    grads = [g.reshape(3, rows, share) for g in give_back(grads)]
    token_grad, grads, norm_gain_grad = unproject(info, x, grad_residual, gain_one, first, grads)
    qkv_grad = dot(normed, grads, 0, 0).astype(low)

    own_sums = table_sums(diagonals.reshape(own_heads, 2 * seq_len), buckets, seq_len)
    sums = lax.dynamic_update_slice_in_dim(jnp.zeros((buckets, heads), jnp.float32), own_sums, c * own_heads, 1)
    side = jnp.stack([wide(norm_gain_grad.reshape(n_fsdp, shard)), wide(ffn_gain_grad.reshape(n_fsdp, shard)), wide(sums.reshape(n_fsdp, small))], axis=1)
    side = jnp.pad(side.astype(low), ((0, 0), (0, shard - 3), (0, 0))).reshape(n_fsdp * shard, 128)
    if remote:
        side, qkv_grad = scatter_all([side, qkv_grad], 2)
    else:
        side, qkv_grad = scatter_rows(side), scatter_rows(qkv_grad)

    full = jnp.float32
    side = side.astype(full)
    qkv_grad = qkv_grad.astype(full)
    feed_grad = feed_grad.astype(full)
    inner_grad = feed_grad[:, width : width + hidden_width].reshape(shard, slabs, n_fsdp, shard).transpose(0, 2, 1, 3).reshape(shard, hidden_width)
    outer_grad = feed_grad[:, width + hidden_width :].reshape(shard, slabs, width).transpose(1, 0, 2).reshape(slabs * shard, width)
    return (layer_out.reshape(tokens.shape), token_grad.reshape(tokens.shape), side[0, :shard], qkv_grad[:, :width], qkv_grad[:, width : 2 * width],
            qkv_grad[:, 2 * width :], feed_grad[:, :width], side[1, :shard], inner_grad, outer_grad, side[2, :small].reshape(bias_table.shape))


def solution(mesh):
    rows = P("fsdp", "ctx", None)
    in_specs = (rows, rows, P("fsdp"), P("fsdp"), P("fsdp", None), P("fsdp", None), P("fsdp", None), P("fsdp", None),
                P("fsdp"), P("fsdp", None), P("fsdp", None), P("fsdp", None))
    out_specs = (rows, rows, P("fsdp"), P("fsdp", None), P("fsdp", None), P("fsdp", None), P("fsdp", None),
                 P("fsdp"), P("fsdp", None), P("fsdp", None), P("fsdp", None))
    return jax.shard_map(per_device, mesh=mesh, in_specs=in_specs, out_specs=out_specs, check_vma=False)
```

```python
import functools

import jax
import jax.numpy as jnp
import numpy as np
from jax import lax
from jax.experimental import pallas as pl
from jax.experimental.pallas import tpu as pltpu
from jax.sharding import PartitionSpec as P

LOG2E = 1.4426950408889634
LN2 = 0.6931471805599453
NEG = -1e30
TILE = 256
QT = 256
HEAD_DIM = 64
EPS = 1e-6
GELU = 0.7978845608028654
CUBIC = 0.044715
VMEM_LIMIT = 60 << 20
CHIPS = (4, 2, 2)
PIECE = 1664


def dot(a, b, ca, cb, precision=None):
    return lax.dot_general(a, b, (((ca,), (cb,)), ((), ())), precision=precision, preferred_element_type=jnp.float32)


def offsets(c, parts, block):
    return [pl.ds(pl.multiple_of(lax.rem(c + parts - j, parts) * block, block), block) for j in range(parts)]


def attend_kernel(info_ref, tvec_ref, *refs, seq_len, head_dim, parts):
    pieces, outs = refs[:parts], refs[parts : 2 * parts]
    lse_ref, strip_ref, q_ref, k_ref, v_ref, o_ref = refs[2 * parts :]
    places = offsets(info_ref[0], parts, seq_len // parts)
    for j in range(parts):
        for t, ref in enumerate((q_ref, k_ref, v_ref)):
            ref[places[j], :] = pieces[j][t, 0]

    heads = q_ref.shape[-1] // head_dim
    blocks = seq_len // TILE
    far = seq_len - QT

    @pl.when(pl.program_id(1) == 0)
    def _():
        for h in range(heads):
            wide = jnp.broadcast_to(tvec_ref[0, h : h + 1, :], (QT, tvec_ref.shape[-1]))
            strip_ref[h] = pltpu.roll(wide, 0, 1, stride=1, stride_axis=0)

    live = info_ref[1 + pl.program_id(1)]
    lane = lax.broadcasted_iota(jnp.int32, (1, q_ref.shape[-1]), 1) // head_dim
    column = lax.broadcasted_iota(jnp.int32, (1, TILE), 1)

    def with_blocks(used):
        top = TILE * used
        kept = [lane == h for h in range(heads)]
        keys = [jnp.where(kept[h], k_ref[0:top, :], 0) for h in range(heads)]
        ones = jnp.ones((top, 128), jnp.bfloat16)
        values = [jnp.concatenate([jnp.where(kept[h], v_ref[0:top, :], 0), ones], axis=1) for h in range(heads)]

        def query_tile(a, carry):
            here = pl.ds(pl.multiple_of(a * QT, QT), QT)
            q = q_ref[here, :]
            total = None
            for h in range(heads):
                at = pl.ds(pl.multiple_of(far - QT * a, TILE), top)
                scores = dot(q, keys[h], 1, 1) + strip_ref[h, :, at]
                last = jnp.where(column + (top - TILE) < live, scores[:, top - TILE :], NEG)
                scores = jnp.concatenate([scores[:, : top - TILE], last], axis=1) if used > 1 else last
                peak = jnp.max(scores, axis=1, keepdims=True)
                probs = jnp.exp2(scores - peak).astype(jnp.bfloat16)
                out = dot(probs, values[h], 1, 0)
                mass = out[:, 128:]
                out = out[:, :128] * (1.0 / mass)
                total = out if total is None else total + out
                lse = peak + jnp.log2(mass)
                both = lse if h == 0 else jnp.where(kept[h], lse, both)
            both = jnp.transpose(both)
            for h in range(heads):
                lse_ref[0, 0, h : h + 1, here] = both[h * head_dim : h * head_dim + 1, :]
            o_ref[here, :] = total.astype(jnp.bfloat16)
            return carry

        lax.fori_loop(0, seq_len // QT, query_tile, 0, unroll=True)

    for used in range(1, blocks + 1):
        pl.when((live + TILE - 1) // TILE == used)(functools.partial(with_blocks, used))

    for j in range(parts):
        outs[j][0] = o_ref[places[j], :]


def attend(info, tvec, pieces, head_dim):
    parts = len(pieces)
    _, seqs, block, width = pieces[0].shape
    seq_len = block * parts
    pairs = width // 128
    heads = 128 // head_dim
    strip = tvec.shape[-1]
    three = pl.BlockSpec((3, 1, block, 128), lambda p, s, n: (0, s, 0, p))
    one = pl.BlockSpec((1, block, 128), lambda p, s, n: (s, 0, p))
    return pl.pallas_call(
        functools.partial(attend_kernel, seq_len=seq_len, head_dim=head_dim, parts=parts),
        grid_spec=pltpu.PrefetchScalarGridSpec(
            num_scalar_prefetch=1, grid=(pairs, seqs),
            in_specs=[pl.BlockSpec((1, heads, strip), lambda p, s, n: (p, 0, 0))] + [three] * parts,
            out_specs=[one] * parts + [pl.BlockSpec((1, 1, heads, seq_len), lambda p, s, n: (p, s, 0, 0))],
            scratch_shapes=[pltpu.VMEM((heads, QT, strip), jnp.float32)] + [pltpu.VMEM((seq_len, 128), jnp.bfloat16)] * 4),
        out_shape=[jax.ShapeDtypeStruct((seqs, block, width), jnp.bfloat16)] * parts + [jax.ShapeDtypeStruct((pairs, seqs, heads, seq_len), jnp.float32)],
        compiler_params=pltpu.CompilerParams(vmem_limit_bytes=VMEM_LIMIT),
        cost_estimate=pl.CostEstimate(flops=16 * seqs * width * seq_len * seq_len, bytes_accessed=8 * seqs * seq_len * width, transcendentals=0),
        name="attend",
    )(info, tvec, *pieces)


def unattend_kernel(info_ref, tvec_ref, *refs, seq_len, head_dim, parts):
    pieces, out_pieces, do_pieces = refs[:parts], refs[parts : 2 * parts], refs[2 * parts : 3 * parts]
    lse_ref = refs[3 * parts]
    grads, dt_ref = refs[3 * parts + 1 : 4 * parts + 1], refs[4 * parts + 1]
    strip_ref, sums_ref, dk_acc, dv_acc, q_ref, k_ref, v_ref, o_ref, do_ref, dq_ref = refs[4 * parts + 2 :]
    places = offsets(info_ref[0], parts, seq_len // parts)
    for j in range(parts):
        for t, ref in enumerate((q_ref, k_ref, v_ref)):
            ref[places[j], :] = pieces[j][t, 0]
        o_ref[places[j], :] = out_pieces[j][0]
        do_ref[places[j], :] = do_pieces[j][0]
    heads = q_ref.shape[-1] // head_dim
    blocks = seq_len // TILE
    far = seq_len - TILE
    bands = (2 * blocks - 1) * TILE

    @pl.when(pl.program_id(1) == 0)
    def _():
        for h in range(heads):
            wide = jnp.broadcast_to(tvec_ref[0, h : h + 1, :], (TILE, tvec_ref.shape[-1]))
            wide = pltpu.roll(wide, 0, 1, stride=1, stride_axis=0)
            for b in range(2 * blocks - 1):
                strip_ref[TILE * b : TILE * (b + 1), TILE * h : TILE * (h + 1)] = jnp.transpose(wide[:, TILE * b : TILE * (b + 1)])
        sums_ref[...] = jnp.zeros_like(sums_ref)

    live = info_ref[1 + pl.program_id(1)]
    lane = lax.broadcasted_iota(jnp.int32, (1, q_ref.shape[-1]), 1) // head_dim
    row = lax.broadcasted_iota(jnp.int32, (TILE, 1), 0)
    kept = [lane == h for h in range(heads)]

    def with_blocks(used):
        top = TILE * used
        dk_acc[0:top, :] = jnp.zeros((top, dk_acc.shape[1]), jnp.float32)
        dv_acc[0:top, :] = jnp.zeros((top, dv_acc.shape[1]), jnp.float32)

        def query_tile(a, carry):
            here = pl.ds(pl.multiple_of(a * TILE, TILE), TILE)
            q = q_ref[here, :]
            do = do_ref[here, :]
            product = jnp.transpose(do.astype(jnp.float32) * o_ref[here, :].astype(jnp.float32))
            qs = jnp.concatenate([jnp.where(kept[h], q, 0) for h in range(heads)], axis=0)
            dos = jnp.concatenate([jnp.where(kept[h], do, 0) for h in range(heads)], axis=0)
            delta = jnp.concatenate([jnp.sum(product[h * head_dim : (h + 1) * head_dim], axis=0, keepdims=True) for h in range(heads)], axis=1)
            lse = jnp.concatenate([lse_ref[0, 0, h : h + 1, here] for h in range(heads)], axis=1)
            at = pl.ds(pl.multiple_of(far - TILE * a, TILE), top)
            kb = k_ref[0:top, :]
            vb = v_ref[0:top, :]
            p = jnp.exp2(dot(kb, qs, 1, 1) + strip_ref[at, :] - lse)
            last = jnp.where(row + (top - TILE) < live, p[top - TILE :], 0.0)
            p = jnp.concatenate([p[: top - TILE], last], axis=0) if used > 1 else last
            ds = p * (dot(vb, dos, 1, 1) - delta)
            sums_ref[at, :] += ds
            p = p.astype(jnp.bfloat16)
            ds = ds.astype(jnp.bfloat16)
            dv_acc[0:top, :] += dot(p, dos, 1, 0)
            dk_acc[0:top, :] += dot(ds, qs, 1, 0)
            dq = dot(ds, kb, 0, 0)
            dq_total = dq[0:TILE]
            for h in range(1, heads):
                dq_total = jnp.where(kept[h], dq[TILE * h : TILE * (h + 1)], dq_total)
            dq_ref[here, :] = (dq_total * LN2).astype(jnp.bfloat16)
            return carry

        lax.fori_loop(0, used, query_tile, 0, unroll=2)
        if used < blocks:
            dq_ref[top:, :] = jnp.zeros((seq_len - top, q_ref.shape[-1]), jnp.bfloat16)
            dk_acc[top:, :] = jnp.zeros((seq_len - top, q_ref.shape[-1]), jnp.float32)
            dv_acc[top:, :] = jnp.zeros((seq_len - top, q_ref.shape[-1]), jnp.float32)

    for used in range(1, blocks + 1):
        pl.when((live + TILE - 1) // TILE == used)(functools.partial(with_blocks, used))

    for j in range(parts):
        grads[j][0, 0] = dq_ref[places[j], :]
        grads[j][1, 0] = dk_acc[places[j], :].astype(jnp.bfloat16)
        grads[j][2, 0] = dv_acc[places[j], :].astype(jnp.bfloat16)

    @pl.when(pl.program_id(1) == pl.num_programs(1) - 1)
    def _():
        wide = dt_ref.shape[-1]
        for h in range(heads):
            turned = jnp.concatenate([jnp.transpose(sums_ref[TILE * b : TILE * (b + 1), TILE * h : TILE * (h + 1)]) for b in range(2 * blocks - 1)]
                                     + [jnp.zeros((TILE, wide - bands), jnp.float32)], axis=1)
            group = turned[0:8]
            for g in range(1, TILE // 8):
                group = group + pltpu.roll(turned[8 * g : 8 * (g + 1)], wide - 8 * g, 1)
            diagonal = group[0:1]
            for s in range(1, 8):
                diagonal = diagonal + pltpu.roll(group[s : s + 1], wide - s, 1)
            dt_ref[0, h : h + 1, :] = diagonal


def unattend(info, tvec, pieces, outs, do, lse, head_dim):
    parts = len(pieces)
    _, seqs, block, width = pieces[0].shape
    seq_len = block * parts
    pairs = width // 128
    heads = 128 // head_dim
    strip = tvec.shape[-1]
    bands = 2 * seq_len - TILE
    three = pl.BlockSpec((3, 1, block, 128), lambda p, s, n: (0, s, 0, p))
    one = pl.BlockSpec((1, block, 128), lambda p, s, n: (s, 0, p))
    vec = pl.BlockSpec((1, heads, strip), lambda p, s, n: (p, 0, 0))
    return pl.pallas_call(
        functools.partial(unattend_kernel, seq_len=seq_len, head_dim=head_dim, parts=parts),
        grid_spec=pltpu.PrefetchScalarGridSpec(
            num_scalar_prefetch=1, grid=(pairs, seqs),
            in_specs=[vec] + [three] * parts + [one] * (2 * parts) + [pl.BlockSpec((1, 1, heads, seq_len), lambda p, s, n: (p, s, 0, 0))],
            out_specs=[three] * parts + [vec],
            scratch_shapes=[pltpu.VMEM((bands, heads * TILE), jnp.float32), pltpu.VMEM((bands, heads * TILE), jnp.float32),
                            pltpu.VMEM((seq_len, 128), jnp.float32), pltpu.VMEM((seq_len, 128), jnp.float32)]
            + [pltpu.VMEM((seq_len, 128), jnp.bfloat16)] * 6),
        out_shape=[jax.ShapeDtypeStruct((3, seqs, block, width), jnp.bfloat16)] * parts + [jax.ShapeDtypeStruct((pairs, heads, strip), jnp.float32)],
        compiler_params=pltpu.CompilerParams(vmem_limit_bytes=VMEM_LIMIT),
        cost_estimate=pl.CostEstimate(flops=40 * seqs * width * seq_len * seq_len, bytes_accessed=16 * seqs * seq_len * width, transcendentals=0),
        name="unattend",
    )(info, tvec, *pieces, *outs, *do, lse)


def bucket_edges():
    distance = np.arange(1, 512)
    scaled = 8 + np.floor(np.log(distance / 8.0) / np.log(16.0) * 8.0)
    level = np.where(distance < 8, distance, np.minimum(15, scaled))
    return np.array([distance[level >= target][0] for target in range(1, 16)], np.int32)

def levels_of(offset):
    level = jnp.sum((jnp.abs(offset)[:, None] >= jnp.asarray(bucket_edges())).astype(jnp.int32), axis=1)
    return level + 16 * (offset > 0).astype(jnp.int32)

def bias_vectors(table, seq_len, tile=TILE):
    x = jnp.arange(2 * seq_len, dtype=jnp.int32)
    far = seq_len - tile
    offset = jnp.where(x < 2 * seq_len - tile, x - far, x - far - 2 * seq_len)
    onehot = (levels_of(offset)[:, None] == jnp.arange(table.shape[0])).astype(jnp.float32)
    return jnp.einsum("xb,bh->hx", onehot, table.astype(jnp.float32) * LOG2E, precision=lax.Precision.HIGHEST)

def table_sums(diag, buckets, seq_len):
    x = jnp.arange(2 * seq_len, dtype=jnp.int32)
    far = seq_len - TILE
    offset = jnp.where(x < 2 * seq_len - TILE, x - far, x - far - 2 * seq_len)
    onehot = ((levels_of(offset)[:, None] == jnp.arange(buckets)) & (jnp.abs(offset) < seq_len)[:, None]).astype(jnp.float32)
    return jnp.einsum("zb,hz->bh", onehot, diag, precision=lax.Precision.HIGHEST)


class Place:
    def __init__(self):
        c = lax.axis_index("ctx")
        f = lax.axis_index("fsdp")
        self.c = c
        self.other = 1 - c
        z, y, x = f // 4, (f // 2) % 2, f % 2
        self.z, self.up, self.down, self.far = z, (z + 1) % 4, (z + 3) % 4, (z + 2) % 4
        self.own = (y, x)
        self.u = ((y + c) % 2, (x + 1 - c) % 2)
        self.w = ((y + 1 - c) % 2, (x + c) % 2)
        self.uw = (1 - y, 1 - x)
        flat = lambda zz, col: {"fsdp": zz * 4 + col[0] * 2 + col[1]}
        self.to = {"u": flat(z, self.u), "w": flat(z, self.w), "up": flat(self.up, self.own),
                   "down": flat(self.down, self.own), "core": {"ctx": 1 - c}}

    def greet(self):
        barrier = pltpu.get_barrier_semaphore()
        for target in self.to.values():
            pl.semaphore_signal(barrier, inc=1, device_id=target, device_id_type=pl.DeviceIdType.MESH)
        pl.semaphore_wait(barrier, len(self.to))


class Copies:
    def __init__(self, place, send, recv):
        self.place, self.send, self.recv = place, send, recv
        self.made = {}

    def start(self, name, ends, to):
        self.made[name] = (len(self.made), ends, to)
        self.copy(name).start()

    def copy(self, name):
        i, ends, to = self.made[name]
        src, dst = ends()
        return pltpu.make_async_remote_copy(src_ref=src, dst_ref=dst, send_sem=self.send.at[i], recv_sem=self.recv.at[i],
                                            device_id=self.place.to[to], device_id_type=pl.DeviceIdType.MESH)

    def arrived(self, name):
        self.copy(name).wait_recv()

    def finish(self):
        for name in self.made:
            self.copy(name).wait_send()


def windows(columns, size):
    cuts = list(range(0, columns, size))
    if len(cuts) > 1 and columns - cuts[-1] < size // 2:
        cuts.pop()
    return [(a, b - a) for a, b in zip(cuts, cuts[1:] + [columns])]


def gather_steps(i, shard, out, window, place, copies, local):
    p = place
    columns = pl.ds(*window)
    name = lambda s: (i, s)
    levels = [p.z, p.down, p.far, p.up]
    at = lambda k, col: out.at[levels[k], col[0], col[1], p.c, :, columns]
    mine = shard.at[p.c, :, columns]
    theirs = shard.at[p.other, :, columns]
    kept = [pltpu.make_async_copy(mine, at(0, p.own), local.at[2 * i]),
            pltpu.make_async_copy(theirs, out.at[p.z, p.own[0], p.own[1], p.other, :, columns], local.at[2 * i + 1])]

    def own(k):
        if k == 0:
            for copy in kept:
                copy.start()
        else:
            copies.arrived(name("z %d" % k))
        source = mine if k == 0 else at(k, p.own)
        if k < 3:
            copies.start(name("z %d" % (k + 1)), lambda: (source, at(k, p.own)), "up")
        copies.start(name("u %d" % k), lambda: (source, at(k, p.own)), "u")
        copies.start(name("w own %d" % k), lambda: (source, at(k, p.own)), "w")
        if k > 0:
            copies.start(name("core own %d" % k), lambda: (source, at(k, p.own)), "core")

    def turn(k):
        copies.arrived(name("u %d" % k))
        copies.start(name("w u %d" % k), lambda: (at(k, p.u), at(k, p.u)), "w")
        copies.start(name("core u %d" % k), lambda: (at(k, p.u), at(k, p.u)), "core")

    def across(k):
        copies.arrived(name("w own %d" % k))
        copies.start(name("core w %d" % k), lambda: (at(k, p.w), at(k, p.w)), "core")
        copies.arrived(name("w u %d" % k))
        copies.start(name("core uw %d" % k), lambda: (at(k, p.uw), at(k, p.uw)), "core")

    def end():
        for k in range(4):
            for what in ("own", "u", "w", "uw"):
                if k > 0 or what != "own":
                    copies.arrived(name("core %s %d" % (what, k)))
        for copy in kept:
            copy.wait()

    def step(n):
        if n < 4:
            own(n)
        if 0 <= n - 1 < 4:
            turn(n - 1)
        if 0 <= n - 2 < 4:
            across(n - 2)

    return [functools.partial(step, n) for n in range(6)] + [end]


GATHER_COPIES = 3 + 4 + 8 + 15


def lockstep(chains):
    def run(step):
        for i, chain in enumerate(chains):
            if 0 <= step - i < len(chain):
                chain[step - i]()

    return [functools.partial(run, step) for step in range(len(chains) - 1 + max(len(chain) for chain in chains))]


def staggered(chains):
    for step in lockstep(chains):
        step()


def gather_kernel(*refs, count):
    shards, outs = refs[:count], refs[count : 2 * count]
    send, recv, local = refs[2 * count :]
    place = Place()
    place.greet()
    copies = Copies(place, send, recv)
    parts = [(i, window) for i in range(count) for window in windows(shards[i].shape[-1], PIECE)]
    staggered([gather_steps(n, shards[i], outs[i], window, place, copies, local) for n, (i, window) in enumerate(parts)])
    copies.finish()


def gather_all(shards, collective_id):
    split = [s.reshape(2, s.shape[0] // 2, s.shape[1]) for s in shards]
    count = len(shards)
    parts = sum(len(windows(s.shape[-1], PIECE)) for s in split)
    anywhere = pl.BlockSpec(memory_space=pl.ANY)
    outs = pl.pallas_call(
        functools.partial(gather_kernel, count=count),
        in_specs=[anywhere] * count,
        out_specs=[anywhere] * count,
        out_shape=[jax.ShapeDtypeStruct(CHIPS + s.shape, s.dtype) for s in split],
        scratch_shapes=[pltpu.SemaphoreType.DMA((GATHER_COPIES * parts,)), pltpu.SemaphoreType.DMA((GATHER_COPIES * parts,)),
                        pltpu.SemaphoreType.DMA((2 * parts,))],
        compiler_params=pltpu.CompilerParams(collective_id=collective_id, has_side_effects=True),
        name="gather_rows",
    )(*split)
    return [o.reshape(-1, o.shape[-1]) for o in outs]


def add_into(acc, came):
    lead = acc.shape[:-2]
    total = int(np.prod(lead))
    if total == 1:
        index = (0,) * len(lead)
        acc[index] = acc[index] + came[index]
        return

    def body(n, carry):
        index = []
        for extent in reversed(lead):
            index.append(n % extent)
            n = n // extent
        index = tuple(reversed(index))
        acc[index] = acc[index] + came[index]
        return carry

    lax.fori_loop(0, total, body, 0)


def scatter_buffers(rows, columns):
    shapes = [(4, 2, 2), (4, 2, 2), (2, 4), (4,), (3,)]
    return [pltpu.VMEM(lead + (rows, columns), jnp.bfloat16) for lead in shapes]


SCATTER_BUFFERS = 5
SCATTER_COPIES = 1 + 2 + 1 + 3 + 1


def scatter_steps(i, grad, out, window, buffers, place, copies, local):
    p = place
    acc, came, by_w, by_u, by_z = buffers
    columns = pl.ds(*window)
    name = lambda s: (i, s)
    line = lambda col: acc.at[:, col[0], col[1]]
    at = lambda z: acc.at[z, p.own[0], p.own[1]]
    load = lambda: pltpu.make_async_copy(grad.at[:, :, :, p.c, :, columns], acc, local.at[i])

    def first():
        load().start()
        copies.start(name("core"), lambda: (grad.at[:, :, :, p.other, :, columns], came), "core")

    def second():
        load().wait()
        copies.arrived(name("core"))
        add_into(line(p.uw), came.at[:, p.uw[0], p.uw[1]])
        copies.start(name("w 1"), lambda: (line(p.uw), by_w.at[1]), "w")
        add_into(line(p.w), came.at[:, p.w[0], p.w[1]])
        copies.start(name("w 0"), lambda: (line(p.w), by_w.at[0]), "w")
        add_into(line(p.u), came.at[:, p.u[0], p.u[1]])
        add_into(line(p.own), came.at[:, p.own[0], p.own[1]])

    def third():
        copies.arrived(name("w 1"))
        add_into(line(p.u), by_w.at[1])
        copies.start(name("u"), lambda: (line(p.u), by_u), "u")
        copies.arrived(name("w 0"))
        add_into(line(p.own), by_w.at[0])

    def fourth():
        copies.arrived(name("u"))
        add_into(line(p.own), by_u)
        copies.start(name("z 0"), lambda: (at(p.down), by_z.at[0]), "up")

    def climb(k, level):
        def run():
            copies.arrived(name("z %d" % k))
            add_into(at(level), by_z.at[k])
            copies.start(name("z %d" % (k + 1)), lambda: (at(level), by_z.at[k + 1]), "up")
        return run

    def last():
        copies.arrived(name("z 2"))
        out[p.c, :, columns] = at(p.z)[...] + by_z[2]
        copies.start(name("out"), lambda: (out.at[p.c, :, columns], out.at[p.c, :, columns]), "core")

    def end():
        copies.arrived(name("out"))

    return [first, second, third, fourth, climb(0, p.far), climb(1, p.up), last, end]


def inverse_root(v):
    return lax.rsqrt(jnp.mean(v * v, axis=-1, keepdims=True) + EPS)


def norm_back(v, c, gain, e):
    scaled = e * v * c
    down = c * gain * e - v * (c * c) * jnp.mean(gain * scaled, axis=-1, keepdims=True)
    return down, jnp.sum(scaled, axis=0, keepdims=True)


def gelu_pair(u):
    square = u * u
    t = jnp.tanh(u * (GELU + GELU * CUBIC * square))
    half = 0.5 * u
    slope = 0.5 + 0.5 * t + half * (1.0 - t * t) * (GELU + 3.0 * GELU * CUBIC * square)
    return half + half * t, slope


def group(c, j, parts):
    return lax.rem(c + j, parts)


def resident(shape):
    return pl.BlockSpec(shape, lambda i, n: (0,) * len(shape), pipeline_mode=pl.Buffered(1))


def tiles(shape, axis):
    at = lambda i, n: tuple(i if a == axis else 0 for a in range(len(shape)))
    return pl.BlockSpec(shape, at)


def params():
    return pltpu.CompilerParams(vmem_limit_bytes=VMEM_LIMIT)


def cost(flops, size):
    return pl.CostEstimate(flops=int(flops), bytes_accessed=int(size), transcendentals=0)


def project_kernel(info_ref, x_ref, gain_ref, w_ref, normed_ref, *outs, parts):
    c = info_ref[0]
    x = x_ref[...].astype(jnp.float32)
    width = x.shape[1]
    share = width // parts
    normed = (x * inverse_root(x) * gain_ref[...]).astype(jnp.bfloat16)
    normed_ref[...] = normed
    for j in reversed(range(parts)):
        for t in range(3):
            at = pl.ds(pl.multiple_of(t * width + group(c, j, parts) * share, 128), share)
            y = dot(normed, w_ref[:, at], 1, 0)
            outs[j][t] = (y * LOG2E if t == 1 else y).astype(jnp.bfloat16)


def project(info, x, gain, w, parts):
    rows, width = x.shape
    tile = min(256, rows)
    share = width // parts
    return pl.pallas_call(
        functools.partial(project_kernel, parts=parts),
        grid_spec=pltpu.PrefetchScalarGridSpec(
            num_scalar_prefetch=1, grid=(rows // tile,),
            in_specs=[tiles((tile, width), 0), resident((1, width)), resident(w.shape)],
            out_specs=[tiles((tile, width), 0)] + [tiles((3, tile, share), 1)] * parts),
        out_shape=[jax.ShapeDtypeStruct((rows, width), jnp.bfloat16)] + [jax.ShapeDtypeStruct((3, rows, share), jnp.bfloat16)] * parts,
        compiler_params=params(),
        cost_estimate=cost(6 * rows * width * width, 10 * rows * width + 6 * width * width),
        name="project",
    )(info, x, gain, w)


def feed_kernel(info_ref, x_ref, cot_ref, gain_ref, w_ref, *refs, parts, block):
    mixed = refs[:parts]
    mixed_ref, normed_ref, hidden_ref, layer_ref, grad_ref, inner_ref, residual_ref, low_ref, gain_grad_ref = refs[parts : parts + 9]
    grads = refs[parts + 9 : 2 * parts + 9]
    slope_ref = refs[2 * parts + 9]
    c = info_ref[0]
    tile, width = x_ref.shape
    share = width // parts
    chunk = w_ref.shape[0]
    hidden_width = (w_ref.shape[1] - chunk) // 2
    wo = slice(2 * hidden_width, w_ref.shape[1])
    low = jnp.bfloat16
    rows_of = [pl.ds(pl.multiple_of(group(c, j, parts) * share, 128), share) for j in range(parts)]

    residual = x_ref[...].astype(jnp.float32)
    for j in range(parts):
        mixed_ref[:, rows_of[j]] = mixed[j][...]
        residual = residual + dot(mixed[j][...], w_ref[rows_of[j], wo], 1, 0)
    root = inverse_root(residual)
    gain = gain_ref[...]
    normed = (residual * root * gain).astype(low)
    normed_ref[...] = normed
    layer = None
    for k in range(0, hidden_width, chunk):
        value, slope = gelu_pair(dot(normed, w_ref[:, k : k + chunk], 1, 0))
        value = value.astype(low)
        hidden_ref[:, k : k + chunk] = value
        slope_ref[:, k : k + chunk] = slope.astype(slope_ref.dtype)
        part = dot(value, w_ref[:, hidden_width + k : hidden_width + k + chunk], 1, 0)
        layer = part if layer is None else layer + part
    layer_ref[...] = (residual + layer).astype(low)

    start = pl.program_id(0) * tile
    position = c * block + lax.rem(start, block) + lax.broadcasted_iota(jnp.int32, (tile, 1), 0)
    grad = jnp.where(position < info_ref[1 + start // block], cot_ref[...], 0)
    grad_ref[...] = grad
    up = None
    for k in range(0, hidden_width, chunk):
        inner = (dot(grad, w_ref[:, hidden_width + k : hidden_width + k + chunk], 1, 1) * slope_ref[:, k : k + chunk].astype(jnp.float32)).astype(low)
        inner_ref[:, k : k + chunk] = inner
        part = dot(inner, w_ref[:, k : k + chunk], 1, 1)
        up = part if up is None else up + part
    down, gain_grad = norm_back(residual, root, gain, up)

    @pl.when(pl.program_id(0) == 0)
    def _():
        gain_grad_ref[...] = jnp.zeros_like(gain_grad_ref)

    gain_grad_ref[...] += gain_grad
    down = down + grad.astype(jnp.float32)
    residual_ref[...] = down
    down = down.astype(low)
    low_ref[...] = down
    for j in range(parts):
        grads[j][...] = dot(down, w_ref[rows_of[j], wo], 1, 1).astype(low)


def feed(info, x, cot, gain, w, mixed, block, tile=256):
    parts = len(mixed)
    rows, width = x.shape
    hidden = (w.shape[1] - width) // 2
    tile = min(tile, block)
    share = width // parts
    t = lambda w: tiles((tile, w), 0)
    low = lambda w: jax.ShapeDtypeStruct((rows, w), jnp.bfloat16)
    return pl.pallas_call(
        functools.partial(feed_kernel, parts=parts, block=block),
        grid_spec=pltpu.PrefetchScalarGridSpec(
            num_scalar_prefetch=1, grid=(rows // tile,),
            in_specs=[t(width), t(width), resident((1, width)), resident(w.shape)] + [t(share)] * parts,
            out_specs=[t(width), t(width), t(hidden), t(width), t(width), t(hidden), t(width), t(width), resident((1, width))] + [t(share)] * parts,
            scratch_shapes=[pltpu.VMEM((tile, hidden), jnp.bfloat16)]),
        out_shape=[low(width), low(width), low(hidden), low(width), low(width), low(hidden), jax.ShapeDtypeStruct((rows, width), jnp.float32), low(width),
                   jax.ShapeDtypeStruct((1, width), jnp.float32)] + [low(share)] * parts,
        compiler_params=params(),
        cost_estimate=cost(rows * width * (8 * hidden + 4 * width), rows * (18 * width + 4 * hidden) + 4 * width * hidden),
        name="feed",
    )(info, x, cot, gain, w, *mixed)


def weigh_qkv_kernel(info_ref, normed_ref, *refs, parts):
    came, out_ref = refs[:parts], refs[parts]
    for j in range(parts):

        @pl.when(pl.program_id(0) // 3 == j)
        def _():
            out_ref[...] = dot(normed_ref[...], came[j][0], 0, 0).astype(jnp.bfloat16)


def weigh_qkv(info, normed, came):
    parts = len(came)
    rows, width = normed.shape
    share = width // parts
    piece = pl.BlockSpec((1, rows, share), lambda i, n: (i % 3, 0, 0))
    return pl.pallas_call(
        functools.partial(weigh_qkv_kernel, parts=parts),
        grid_spec=pltpu.PrefetchScalarGridSpec(
            num_scalar_prefetch=1, grid=(3 * parts,),
            in_specs=[resident((rows, width))] + [piece] * parts,
            out_specs=pl.BlockSpec((width, share), lambda i, n: (0, (i % 3) * parts + (n[0] + i // 3) % parts))),
        out_shape=jax.ShapeDtypeStruct((width, 3 * width), jnp.bfloat16),
        compiler_params=params(),
        cost_estimate=cost(6 * rows * width * width, 8 * rows * width + 6 * width * width),
        name="weigh_qkv",
    )(info, normed, *came)


def settle_tile(x_ref, residual_ref, gain_ref, w_ref, came, token_ref):
    parts = len(came)
    c = lax.axis_index("ctx")
    x = x_ref[...].astype(jnp.float32)
    width = x.shape[1]
    share = width // parts
    up = None
    for j in range(parts):
        for t in range(3):
            at = pl.ds(pl.multiple_of(t * width + group(c, j, parts) * share, 128), share)
            part = dot(came[j][t], w_ref[:, at], 1, 1)
            up = part if up is None else up + part
    down, _ = norm_back(x, inverse_root(x), gain_ref[...], up)
    token_ref[...] = residual_ref[...] + down


def settle_kernel(x_ref, residual_ref, gain_ref, w_ref, *refs, parts, count, tiled):
    came, grads, token_ref, outs = refs[:parts], refs[parts : parts + count], refs[parts + count], refs[parts + count + 1 : parts + 2 * count + 1]
    scratch = refs[parts + 2 * count + 1 :]
    sums, buffers, (send, recv, local) = scratch[:count], scratch[count:-3], scratch[-3:]
    i = pl.program_id(0)
    if count:
        place = Place()
        copies = Copies(place, send, recv)
        windows_of = [(n, window) for n in range(count) for window in windows(grads[n].shape[-1], PIECE)]
        chains = [scatter_steps(k, grads[n], sums[n], window, buffers[SCATTER_BUFFERS * k : SCATTER_BUFFERS * (k + 1)], place, copies, local)
                  for k, (n, window) in enumerate(windows_of)]
        pl.when(i == 0)(place.greet)
        for n, step in enumerate(lockstep(chains)):
            pl.when(i == n)(step)

    @pl.when(i < tiled)
    def _():
        settle_tile(x_ref, residual_ref, gain_ref, w_ref, came, token_ref)

    if count:

        @pl.when(i == pl.num_programs(0) - 1)
        def _():
            copies.finish()
            for n in range(count):
                outs[n][...] = sums[n][...]


def settle(x, residual, gain, w, came, grads, collective_id):
    parts, count = len(came), len(grads)
    rows, width = x.shape
    tile = min(256, rows)
    tiled = rows // tile
    share = width // parts
    split = [g.reshape(CHIPS + (2, g.shape[0] // 32, g.shape[1])) for g in grads]
    pieces = [(g.shape[-2], window[1]) for g in split for window in windows(g.shape[-1], PIECE)]
    steps = max(tiled, len(pieces) + 7) if count else tiled
    at = lambda i: jnp.minimum(i, tiled - 1)
    row = pl.BlockSpec((tile, width), lambda i: (at(i), 0))
    fixed = lambda shape: pl.BlockSpec(shape, lambda i: (0,) * len(shape), pipeline_mode=pl.Buffered(1))
    copied = SCATTER_COPIES * len(pieces)
    semaphores = [pltpu.SemaphoreType.DMA((max(n, 1),)) for n in (copied, copied, len(pieces))]
    extra = dict(collective_id=collective_id, has_side_effects=True) if count else {}
    token, *outs = pl.pallas_call(
        functools.partial(settle_kernel, parts=parts, count=count, tiled=tiled),
        grid=(steps,),
        in_specs=[row, row, fixed((1, width)), fixed(w.shape)] + [pl.BlockSpec((3, tile, share), lambda i: (0, at(i), 0))] * parts
        + [pl.BlockSpec(memory_space=pl.ANY)] * count,
        out_specs=[row] + [fixed(g.shape[3:]) for g in split],
        out_shape=[jax.ShapeDtypeStruct((rows, width), jnp.float32)] + [jax.ShapeDtypeStruct(g.shape[3:], g.dtype) for g in split],
        scratch_shapes=[pltpu.VMEM(g.shape[3:], g.dtype) for g in split] + [b for p in pieces for b in scatter_buffers(*p)] + semaphores,
        compiler_params=pltpu.CompilerParams(vmem_limit_bytes=VMEM_LIMIT, **extra),
        cost_estimate=cost(6 * rows * width * width, 16 * rows * width + 6 * width * width),
        name="settle",
    )(x, residual, gain, w, *came, *split)
    return token, [o.reshape(-1, o.shape[-1]) for o in outs]


def weigh_kernel(mixed_ref, low_ref, normed_ref, grad_ref, inner_ref, hidden_ref, out_ref, made_ref, came_ref, send, recv, *, slabs):
    s = pl.program_id(0)
    c = lax.axis_index("ctx")
    other = {"ctx": 1 - c}
    total = 2 * slabs + 1

    def copy(k):
        return pltpu.make_async_remote_copy(src_ref=made_ref.at[lax.rem(k, 2), :, 1 - c], dst_ref=came_ref.at[k], send_sem=send.at[k], recv_sem=recv.at[k],
                                            device_id=other, device_id_type=pl.DeviceIdType.MESH)

    @pl.when(s == 0)
    def _():
        barrier = pltpu.get_barrier_semaphore()
        pl.semaphore_signal(barrier, inc=1, device_id=other, device_id_type=pl.DeviceIdType.MESH)
        pl.semaphore_wait(barrier, 1)

    def make(left, right):
        slab = dot(left[...], right[...], 0, 0).astype(jnp.bfloat16)
        made_ref[lax.rem(s, 2)] = slab.reshape(made_ref.shape[1:])
        copy(s).start()

    pl.when(s == 0)(lambda: make(mixed_ref, low_ref))
    pl.when((s > 0) & (s <= slabs))(lambda: make(normed_ref, inner_ref))
    pl.when((s > slabs) & (s < total))(lambda: make(hidden_ref, grad_ref))

    @pl.when(s > 0)
    def _():
        earlier = copy(s - 1)
        earlier.wait_recv()
        out_ref[...] = made_ref[lax.rem(s - 1, 2), :, c] + came_ref[s - 1]
        earlier.wait_send()


def weigh(mixed, low, normed, grad, inner, hidden, chips, collective_id):
    rows, width = mixed.shape
    slabs = hidden.shape[1] // width
    total = 2 * slabs + 1
    part = width // chips // 2
    whole = pl.BlockSpec((rows, width), lambda s: (0, 0), pipeline_mode=pl.Buffered(1))
    slab = lambda first: pl.BlockSpec((rows, width), lambda s: (0, jnp.clip(s - first, 0, slabs - 1)))
    return pl.pallas_call(
        functools.partial(weigh_kernel, slabs=slabs),
        grid=(total + 1,),
        in_specs=[whole, whole, whole, whole, slab(1), slab(1 + slabs)],
        out_specs=pl.BlockSpec((chips, part, width), lambda s: (0, 0, jnp.maximum(s - 1, 0))),
        out_shape=jax.ShapeDtypeStruct((chips, part, total * width), jnp.bfloat16),
        scratch_shapes=[pltpu.VMEM((2, chips, 2, part, width), jnp.bfloat16), pltpu.VMEM((total, chips, part, width), jnp.bfloat16),
                        pltpu.SemaphoreType.DMA((total,)), pltpu.SemaphoreType.DMA((total,))],
        compiler_params=pltpu.CompilerParams(collective_id=collective_id, has_side_effects=True, vmem_limit_bytes=VMEM_LIMIT),
        cost_estimate=cost(2 * rows * width * width * total, 2 * rows * width * 13),
        name="weigh",
    )(mixed, low, normed, grad, inner, hidden)


def gather_rows(shard):
    n = lax.axis_size("ctx")
    part = shard.shape[0] // n
    mine = lax.dynamic_slice_in_dim(shard, lax.axis_index("ctx") * part, part, 0)
    return lax.all_gather(mine, ("fsdp", "ctx"), axis=0, tiled=True)


def scatter_rows(grad):
    part = lax.psum_scatter(grad, ("fsdp", "ctx"), scatter_dimension=0, tiled=True)
    return lax.all_gather(part, "ctx", axis=0, tiled=True)


def both_halves(part):
    other = lax.ppermute(part, "ctx", [(0, 1), (1, 0)])
    first = lax.axis_index("ctx") == 0
    return jnp.concatenate([jnp.where(first, part, other), jnp.where(first, other, part)], axis=0)


def exchange(pieces):
    n = len(pieces)
    return [pieces[0]] + [lax.ppermute(pieces[j], "ctx", [(i, (i + j) % n) for i in range(n)]) for j in range(1, n)]


def give_back(pieces):
    n = len(pieces)
    return [pieces[0]] + [lax.ppermute(pieces[j], "ctx", [(i, (i - j) % n) for i in range(n)]) for j in range(1, n)]


def wide(x):
    return jnp.pad(x, [(0, 0)] * (x.ndim - 1) + [(0, 128 - x.shape[-1])])


def by_chip(shape):
    return shape == (2, 16)


def per_device(tokens, cotangent, lengths, norm_gain, query_weight, key_weight, value_weight, output_weight,
               ffn_gain, inner_weight, outer_weight, bias_table):
    seqs, block, width = tokens.shape
    rows = seqs * block
    n_ctx = lax.axis_size("ctx")
    n_fsdp = lax.axis_size("fsdp")
    c = lax.axis_index("ctx")
    seq_len = block * n_ctx
    heads = bias_table.shape[1]
    buckets = bias_table.shape[0] * n_fsdp
    shard = query_weight.shape[0]
    hidden_width = inner_weight.shape[1]
    slabs = hidden_width // width
    own_heads = heads // n_ctx
    pairs = own_heads * HEAD_DIM // 128
    per_pair = 128 // HEAD_DIM
    small = bias_table.size
    share = width // n_ctx
    low = jnp.bfloat16
    remote = by_chip((n_ctx, n_fsdp))
    info = jnp.concatenate([jnp.full((1,), c, jnp.int32), lengths])

    inner = inner_weight.reshape(shard, n_fsdp, slabs, shard).transpose(0, 2, 1, 3).reshape(shard, hidden_width)
    outer = outer_weight.reshape(slabs, shard, width).transpose(1, 0, 2).reshape(shard, slabs * width)
    w_feed = gather_rows(jnp.concatenate([inner, outer, output_weight], axis=1))
    side = jnp.stack([wide(norm_gain), wide(ffn_gain), wide(bias_table.reshape(small))])
    side = jnp.pad(side, ((0, shard - 3), (0, 0)))
    first = jnp.concatenate([query_weight, key_weight, value_weight, side], axis=1)
    first = gather_all([first], 1)[0] if remote else gather_rows(first)
    side = first[:, 3 * width :].reshape(n_fsdp, shard, 128)
    gain_one = side[:, 0, :shard].reshape(1, width).astype(jnp.float32)
    gain_two = side[:, 1, :shard].reshape(1, width).astype(jnp.float32)
    table = side[:, 2, :small].reshape(buckets, heads)
    own_table = lax.dynamic_slice_in_dim(table, c * own_heads, own_heads, 1)
    vector_q = bias_vectors(own_table, seq_len, QT).reshape(pairs, per_pair, 2 * seq_len)
    vector_k = bias_vectors(own_table, seq_len, TILE).reshape(pairs, per_pair, 2 * seq_len)

    x = tokens.reshape(rows, width)
    cot = cotangent.reshape(rows, width)
    normed, *qkv = project(info, x, gain_one, first, n_ctx)
    qkv = exchange([p.reshape(3, seqs, block, share) for p in qkv])
    *out, lse = attend(info, vector_q, qkv, HEAD_DIM)
    mixed = [m.reshape(rows, share) for m in give_back(out)]
    (mixed, normed_ffn, hidden, layer_out, grad_out, grad_inner, grad_residual, grad_low, ffn_gain_grad, *grad_mixed) = feed(
        info, x, cot, gain_two, w_feed, mixed, block)
    grad_mixed = exchange([g.reshape(seqs, block, share) for g in grad_mixed])

    if remote:
        feed_grad = weigh(mixed, grad_low, normed_ffn, grad_out, grad_inner, hidden, n_fsdp, 3)
        feed_grad, grad_mixed = lax.optimization_barrier((feed_grad, grad_mixed))
        feed_grad = lax.psum_scatter(feed_grad, "fsdp", scatter_dimension=0, tiled=False)
        feed_grad = both_halves(feed_grad)
    else:
        outer_grad = [dot(hidden[:, q * width : (q + 1) * width], grad_out, 0, 0) for q in range(slabs)]
        feed_grad = jnp.concatenate([dot(mixed, grad_low, 0, 0), dot(normed_ffn, grad_inner, 0, 0)] + outer_grad, axis=1).astype(low)
        feed_grad = scatter_rows(feed_grad)

    *grads, diagonals = unattend(info, vector_k, qkv, out, grad_mixed, lse, HEAD_DIM)
    grads = [g.reshape(3, rows, share) for g in give_back(grads)]
    qkv_grad = weigh_qkv(info, normed, grads)

    own_sums = table_sums(diagonals.reshape(own_heads, 2 * seq_len), buckets, seq_len)
    sums = lax.dynamic_update_slice_in_dim(jnp.zeros((buckets, heads), jnp.float32), own_sums, c * own_heads, 1)
    side = jnp.stack([wide(ffn_gain_grad.reshape(n_fsdp, shard)), wide(sums.reshape(n_fsdp, small))], axis=1)
    side = jnp.pad(side.astype(low), ((0, 0), (0, shard - 2), (0, 0))).reshape(n_fsdp * shard, 128)
    if remote:
        token_grad, (side, qkv_grad) = settle(x, grad_residual, gain_one, first, grads, [side, qkv_grad], 2)
    else:
        token_grad, _ = settle(x, grad_residual, gain_one, first, grads, [], 2)
        side, qkv_grad = scatter_rows(side), scatter_rows(qkv_grad)

    full = jnp.float32
    side = side.astype(full)
    qkv_grad = qkv_grad.astype(full)
    feed_grad = feed_grad.astype(full)
    weights = jnp.concatenate([query_weight, key_weight, value_weight], axis=1).astype(full)
    norm_gain_grad = jnp.sum(weights * qkv_grad, axis=1) / norm_gain.astype(full)
    inner_grad = feed_grad[:, width : width + hidden_width].reshape(shard, slabs, n_fsdp, shard).transpose(0, 2, 1, 3).reshape(shard, hidden_width)
    outer_grad = feed_grad[:, width + hidden_width :].reshape(shard, slabs, width).transpose(1, 0, 2).reshape(slabs * shard, width)
    return (layer_out.reshape(tokens.shape), token_grad.reshape(tokens.shape), norm_gain_grad, qkv_grad[:, :width], qkv_grad[:, width : 2 * width],
            qkv_grad[:, 2 * width :], feed_grad[:, :width], side[0, :shard], inner_grad, outer_grad, side[1, :small].reshape(bias_table.shape))


def solution(mesh):
    rows = P("fsdp", "ctx", None)
    in_specs = (rows, rows, P("fsdp"), P("fsdp"), P("fsdp", None), P("fsdp", None), P("fsdp", None), P("fsdp", None),
                P("fsdp"), P("fsdp", None), P("fsdp", None), P("fsdp", None))
    out_specs = (rows, rows, P("fsdp"), P("fsdp", None), P("fsdp", None), P("fsdp", None), P("fsdp", None),
                 P("fsdp"), P("fsdp", None), P("fsdp", None), P("fsdp", None))
    return jax.shard_map(per_device, mesh=mesh, in_specs=in_specs, out_specs=out_specs, check_vma=False)
```
